512 devices in a mesh: fsdp: 128 (over z, y, core), tp: 4 (over x).
Axes of the slice: x: 4, y: 8, z: 8, core: 2. Of those that a mesh axis runs over, the one named last changes fastest.
Arguments:
- hidden_rows: bfloat16 [32768, 5120], P('fsdp', 'tp'), may hold values from -6 to 6
- cotangent: bfloat16 [32768, 2560], P('fsdp', 'tp'), may hold values from -6 to 6
- norm_gain: float32 [5120], replicated, may hold values from 0.1 to 1.9
- query_weight: bfloat16 [5120, 2560], P('fsdp', 'tp'), may hold values from -4 to 4
- key_weight: bfloat16 [5120, 512], P('fsdp', 'tp'), may hold values from -4 to 4
- value_weight: bfloat16 [5120, 512], P('fsdp', 'tp'), may hold values from -0.078125 to 0.078125
- slot_source: int32 [512], P('fsdp'), may hold values from -1 to 3, as said below
- slot_segment: int32 [512], P('fsdp'), may hold values from -1 to 255, as said below
- slot_position: int32 [512], P('fsdp'), may hold values from 0 to 1, as said below
Outputs:
- attended: bfloat16 [32768, 2560], P('fsdp', 'tp')
- value_grad: float32 [5120, 512], P('fsdp', 'tp')
The draws below stay inside these ranges and needn't reach their ends.
Inputs may be any that keep to these rules, and one draw needn't show every extreme that they name: `slot_source`: -1 marks an empty slot; c < 2 names block c of the learner's own fsdp index, c >= 2 block c - 2 of the index before it (cyclically). Each block is held by at most one slot; some learner has all 4 slots filled; all blocks of one sequence stand on one learner. `slot_segment`: each sequence has one id, unique over the whole rollout (the fsdp index that produced it times 2 plus its first block); -1 marks an empty slot; the largest id occurs in every draw. `slot_position`: the blocks of one sequence have the positions 0, 1, 2 and so on, each once; 0 in an empty slot.
All inputs are finite; a program needn't handle non-finite values.
Results may differ from the reference program's by a relative error of at most 0.0079.
Values may be sent and summed in bfloat16 or wider, within the bound.
A program may use at most 64 MiB of HBM per device.

```python
import jax
import jax.numpy as jnp
from jax import lax

D = 5120
HD = 128
QH = 20
KVH = 4
BLK = 128
GEN_BLK = 2
CAP_BLK = 4
TOKENS = 32768
N_FSDP = 128


def plan_tables(key):
    used_key, break_key, leave_key, order_key = jax.random.split(key, 4)
    blocks = jnp.arange(GEN_BLK, dtype=jnp.int32)
    used = jax.random.randint(used_key, (N_FSDP,), 2, GEN_BLK + 1)
    used = used.at[N_FSDP - 1].set(GEN_BLK).at[0].set(GEN_BLK).at[1].set(GEN_BLK)
    breaks = jax.random.randint(break_key, (N_FSDP, GEN_BLK), 0, 2)
    breaks = breaks.at[:, 0].set(1).at[N_FSDP - 1, GEN_BLK - 1].set(1)
    starts = lax.cummax(jnp.where(breaks == 1, blocks[None, :], 0), axis=1)
    position = blocks[None, :] - starts
    leaving = jax.random.randint(leave_key, (N_FSDP, GEN_BLK), 0, 2)
    leaving = jnp.take_along_axis(leaving, starts, axis=1)
    leaving = leaving.at[0].set(1).at[1].set(0)
    valid = blocks[None, :] < used[:, None]
    stay = valid & (leaving == 0)
    arrive = jnp.roll(valid & (leaving == 1), 1, axis=0)
    wanted = jnp.concatenate([stay, arrive], axis=1)
    row_keys = jnp.arange(N_FSDP, dtype=jnp.int32)[:, None] * GEN_BLK + starts
    keys_all = jnp.concatenate([row_keys, jnp.roll(row_keys, 1, axis=0)], axis=1)
    places_all = jnp.concatenate([position, jnp.roll(position, 1, axis=0)], axis=1)
    ranks = jnp.cumsum(wanted.astype(jnp.int32), axis=1) - 1
    orders = jax.vmap(lambda single: jax.random.permutation(single, 2 * GEN_BLK))(jax.random.split(order_key, N_FSDP))
    inverse = jnp.argsort(orders, axis=1).astype(jnp.int32)
    matches = (ranks[:, None, :] == inverse[:, :, None]) & wanted[:, None, :]
    candidates = jnp.arange(2 * GEN_BLK, dtype=jnp.int32)
    source = jnp.max(jnp.where(matches, candidates[None, None, :], -1), axis=2)
    segment = jnp.max(jnp.where(matches, keys_all[:, None, :], -1), axis=2)
    place = jnp.max(jnp.where(matches, places_all[:, None, :], 0), axis=2)
    return (source.reshape(-1).astype(jnp.int32), segment.reshape(-1).astype(jnp.int32), place.reshape(-1).astype(jnp.int32))


def bounded_normal(key, shape):
    return jnp.clip(jax.random.normal(key, shape, jnp.float32), -4.0, 4.0)


def draw_slot_source(key, part):
    return plan_tables(key)[0]


def draw_slot_segment(key, part):
    return plan_tables(key)[1]


def draw_slot_position(key, part):
    return plan_tables(key)[2]


def draw_query_weight(key, part):
    key = jax.random.fold_in(key, 21)
    own = bounded_normal(key, (D, QH * HD))
    return (own * D ** (-0.5)).astype(jnp.bfloat16)


def draw_key_weight(key, part):
    key = jax.random.fold_in(key, 22)
    own = bounded_normal(key, (D, KVH * HD))
    return (own * D ** (-0.5)).astype(jnp.bfloat16)


def block_scale(own_key, dims, shards, low, top_value):
    factor_of, own = 1.0, jax.random.fold_in(own_key, 6)
    for dim, parts in shards:
        steps = jnp.exp(jax.random.uniform(jax.random.fold_in(own, dim), (parts,), jnp.float32, low / len(shards), top_value / len(shards)))
        factor_of = factor_of * jnp.repeat(steps, dims[dim] // parts).reshape([-1 if axis == dim else 1 for axis in range(len(dims))])
    return factor_of


def normal_values(rng, shape, spread, most, pieces=(), kind=jnp.bfloat16):
    factor_of = block_scale(rng, shape, pieces, -0.22, 0.18) if pieces else 1.0
    drawn = jax.random.normal(rng, shape, jnp.float32) * spread * factor_of
    return jnp.minimum(jnp.maximum(drawn, -most), most).astype(kind)


def setup_inputs(seed: int = 0) -> dict:
    seeds = jax.random.split(jax.random.key(seed), 10)
    hidden_rows = normal_values(seeds[0], (TOKENS, D), 1.0, 6.0, ((0, 128), (1, 4)))
    cotangent = normal_values(seeds[1], (TOKENS, QH * HD), 1.0, 6.0, ((0, 128), (1, 4)))
    norm_gain = jnp.clip(1.0 + 0.18 * jax.random.normal(seeds[2], (D,), jnp.float32), 0.1, 1.9)
    query_weight = draw_query_weight(jax.random.fold_in(seeds[9], 71), 0)
    key_weight = draw_key_weight(jax.random.fold_in(seeds[9], 71), 0)
    value_weight = normal_values(seeds[5], (D, KVH * HD), D ** -0.5, 0.078125, ((0, 128), (1, 4)))
    slot_source = draw_slot_source(jax.random.fold_in(seeds[9], 71), 0)
    slot_segment = draw_slot_segment(jax.random.fold_in(seeds[9], 71), 0)
    slot_position = draw_slot_position(jax.random.fold_in(seeds[9], 71), 0)
    return dict(hidden_rows=hidden_rows, cotangent=cotangent, norm_gain=norm_gain, query_weight=query_weight, key_weight=key_weight, value_weight=value_weight, slot_source=slot_source, slot_segment=slot_segment, slot_position=slot_position)


epsilon = 1e-06

def reference(hidden_rows, cotangent, norm_gain, query_weight, key_weight, value_weight, slot_source, slot_segment, slot_position):
    group = QH // KVH
    slot_rows = CAP_BLK * BLK
    rows_wide = hidden_rows.astype(jnp.float32)
    mean_sq = lax.optimization_barrier(jnp.mean(rows_wide * rows_wide, axis=1, keepdims=True))
    normed = (rows_wide * lax.rsqrt(mean_sq + epsilon) * norm_gain).astype(jnp.bfloat16)
    queries = jnp.dot(normed, query_weight, preferred_element_type=jnp.float32).astype(jnp.bfloat16)
    keys = jnp.dot(normed, key_weight, preferred_element_type=jnp.float32).astype(jnp.bfloat16)
    values = jnp.dot(normed, value_weight, preferred_element_type=jnp.float32).astype(jnp.bfloat16)
    source = slot_source.reshape(N_FSDP, CAP_BLK)
    segment = slot_segment.reshape(N_FSDP, CAP_BLK)
    position = slot_position.reshape(N_FSDP, CAP_BLK)
    learner = jnp.arange(N_FSDP, dtype=jnp.int32)[:, None]
    arriving = source >= GEN_BLK
    owner = jnp.where(arriving, (learner - 1) % N_FSDP, learner)
    block = owner * GEN_BLK + jnp.where(arriving, source - GEN_BLK, source)
    filled = source >= 0
    inside = jnp.arange(BLK, dtype=jnp.int32)
    token = (jnp.where(filled, block, 0)[:, :, None] * BLK + inside[None, None, :]).reshape(N_FSDP, slot_rows)
    target = jnp.where(jnp.repeat(filled, BLK, axis=1), token, TOKENS).reshape(-1)

    def one_learner(inputs):
        rows_index, fill_slots, seg_slots, pos_slots = inputs
        fill_tok = jnp.repeat(fill_slots, BLK)
        seg_tok = jnp.repeat(seg_slots, BLK)
        pos_tok = jnp.repeat(pos_slots, BLK) * BLK + jnp.tile(inside, CAP_BLK)
        allow = fill_tok[:, None] & fill_tok[None, :] & (seg_tok[:, None] == seg_tok[None, :]) & (pos_tok[:, None] >= pos_tok[None, :])
        query_slots = jnp.take(queries, rows_index, axis=0).astype(jnp.float32).reshape(slot_rows, KVH, group, HD)
        key_slots = jnp.take(keys, rows_index, axis=0).astype(jnp.float32).reshape(slot_rows, KVH, HD)
        value_slots = jnp.take(values, rows_index, axis=0).astype(jnp.float32).reshape(slot_rows, KVH, HD)
        cot_slots = jnp.take(cotangent, rows_index, axis=0).astype(jnp.float32).reshape(slot_rows, KVH, group, HD)
        scores = jnp.einsum('qhgd,khd->hgqk', query_slots, key_slots) * HD ** (-0.5)
        masked = jnp.where(allow[None, None], scores, -1e+30)
        row_max = lax.optimization_barrier(jnp.max(masked, axis=3, keepdims=True))
        raised = jnp.where(allow[None, None], jnp.exp(masked - row_max), 0.0)
        denom = lax.optimization_barrier(jnp.sum(raised, axis=3, keepdims=True)) + (1.0 - fill_tok.astype(jnp.float32))[None, None, :, None]
        probs = (raised / denom).astype(jnp.bfloat16).astype(jnp.float32)
        out_slots = jnp.einsum('hgqk,khd->qhgd', probs, value_slots).astype(jnp.bfloat16).reshape(slot_rows, QH * HD)
        value_cot = jnp.einsum('hgqk,qhgd->khd', probs, cot_slots).astype(jnp.bfloat16).reshape(slot_rows, KVH * HD)
        return (out_slots, value_cot)
    out_all, cot_all = lax.map(one_learner, (token, filled, segment, position))
    attended = jnp.zeros((TOKENS, QH * HD), jnp.bfloat16).at[target].set(out_all.reshape(-1, QH * HD), mode='drop')
    value_cot_rows = jnp.zeros((TOKENS, KVH * HD), jnp.bfloat16).at[target].set(cot_all.reshape(-1, KVH * HD), mode='drop')
    value_grad = jnp.dot(normed.T, value_cot_rows, preferred_element_type=jnp.float32)
    return (attended, value_grad)
```

```python
import functools

import jax
import jax.numpy as jnp
from jax import lax
from jax.experimental import pallas as pl
from jax.experimental.pallas import tpu as pltpu
from jax.sharding import PartitionSpec as P

HD = 128
BLK = 128
GEN_BLK = 2
CAP_BLK = 4
NT = 4
NL = 8
NF = 128
CHIP = 80
PART = 40
LINE = NL * CHIP
SLICE = 1280
HEADS = 5
SW = 384
MESH = pl.DeviceIdType.MESH
F32 = jnp.float32
BF16 = jnp.bfloat16

epsilon = 1e-06


def kernel(
    hid, cot, gain, wq, wk, wv, src, seg, pos,
    att, grad,
    W, V, X, N, stage, sib, tab_out, tab_in, qkv, probs, allow, vc,
    R, Rb, SR, H, P1, F, P2,
    sib_s, sib_r, tab_s, tab_r, xs, xr, xfs, xfr,
    p1s, p1r, v1s, v1r, rs, rr, vs, vr, fs, fr, gs, gr,
    ss, sr, q1s, q1r, q2s, q2r,
):
    g = lax.axis_index("fsdp")
    t = lax.axis_index("tp")
    c = g % 2
    y = (g // 2) % NL
    z = g // (2 * NL)
    a = y + c * (z - y)
    b = z + c * (y - z)

    def first(i):
        return ((z + c * (i - z)) * NL + (i + c * (y - i))) * 2 + c

    def second(i):
        return ((i + c * (z - i)) * NL + (y + c * (i - y))) * 2 + c

    sibling = g + 1 - 2 * c
    before = (g + NF - 1) % NF
    other = (g + NF - 1 + 2 * c) % NF
    right, left, across = (t + 1) % NT, (t + NT - 1) % NT, (t + 2) % NT

    barrier = pltpu.get_barrier_semaphore()

    def greet(f, s):
        pl.semaphore_signal(barrier, inc=1, device_id=(f, s), device_id_type=MESH)

    greet(sibling, t)
    greet(other, t)
    greet(g, right)
    greet(g, left)
    for k in range(1, NL):
        greet(first((a + k) % NL), t)
        greet(second((b + k) % NL), t)

    def remote(source, target, send, recv, f, s):
        return pltpu.make_async_remote_copy(
            src_ref=source, dst_ref=target, send_sem=send, recv_sem=recv,
            device_id=(f, s), device_id_type=MESH,
        )

    stream0 = jnp.concatenate([wq[:, : 2 * HD].astype(F32), wk[...].astype(F32)], axis=1)
    stream1 = wq[:, 2 * HD :].astype(F32)
    value_rows = wv[...].astype(F32)
    stage[:, :SW] = jnp.where(c == 0, stream1, stream0)
    stage[:, SW:] = value_rows

    def held(block):
        flag = jnp.int32(0)
        segment = jnp.int32(0)
        place = jnp.int32(0)
        for s in range(CAP_BLK):
            hit = src[s] == block
            flag = flag + jnp.where(hit, 1, 0)
            segment = segment + jnp.where(hit, seg[s], 0)
            place = place + jnp.where(hit, pos[s], 0)
        return flag, segment, place

    row = lax.broadcasted_iota(jnp.int32, (8, 128), 0)
    table = jnp.zeros((8, 128), jnp.int32)
    for block in range(GEN_BLK):
        for item, value in enumerate(held(GEN_BLK + block)):
            table = jnp.where(row == GEN_BLK * item + block, value, table)
    tab_out[...] = table

    pl.semaphore_wait(barrier, 4 + 2 * (NL - 1))

    sib_copy = remote(stage, sib, sib_s, sib_r, sibling, t)
    sib_copy.start()
    x_copies = []
    for d, h in ((0, 0), (1, 1), (0, 1), (1, 0)):
        copy = remote(
            hid.at[pl.ds(BLK * h, BLK)], X.at[t, h], xs.at[d, h], xr.at[d, h], g, (right, left)[d]
        )
        copy.start()
        x_copies.append(copy)
    tab_copy = remote(tab_out, tab_in, tab_s, tab_r, before, t)
    tab_copy.start()

    X[t, 0] = hid[:BLK, :]
    X[t, 1] = hid[BLK:, :]

    sib_copy.wait_recv()
    mine = jnp.where(c == 0, stream0, stream1)
    theirs = sib[:, :SW]
    top = jnp.where(c == 0, mine, theirs)
    bottom = jnp.where(c == 0, theirs, mine)
    W[c, z, y] = jnp.concatenate([top, bottom], axis=0).astype(BF16)
    top = jnp.where(c == 0, value_rows, sib[:, SW:])
    bottom = jnp.where(c == 0, sib[:, SW:], value_rows)

    @pl.when(c == 0)
    def _():
        V[z, y] = jnp.concatenate([top, bottom], axis=0).astype(BF16)

    p1 = []
    for k in (1, 7, 2, 6, 3, 5, 4):
        copy = remote(
            W.at[c, z, y], W.at[c, z, y], p1s.at[k], p1r.at[k], first((a + k) % NL), t
        )
        copy.start()
        p1.append(copy)
    v1 = []

    @pl.when(c == 0)
    def _():
        for k in (1, 7, 2, 6, 3, 5, 4):
            remote(
                V.at[z, y], V.at[z, y], v1s.at[k], v1r.at[k], first((a + k) % NL), t
            ).start()

    for copy in p1:
        copy.wait_recv()

    def piece(core, line, h):
        items = pl.ds(4 * h, 4)
        return W.at[0, line, items] if core == 0 else W.at[1, items, line]

    def each_core(body):
        for core in range(2):

            @pl.when(c == core)
            def _(core=core):
                body(core)

    def ring(core, d, s, h):
        line = (b + (NL - s, s)[d]) % NL
        ref = piece(core, line, h)
        target = second((b + (1, NL - 1)[d]) % NL)
        return remote(ref, ref, rs.at[d, s, h], rr.at[d, s, h], target, t)

    def arrival(core, d, s, h):
        line = (b + (NL - s, s)[d]) % NL
        ref = piece(core, line, h)
        target = second((b + (1, NL - 1)[d]) % NL)
        return remote(ref, ref, rs.at[d, s - 1, h], rr.at[d, s - 1, h], target, t)

    def to_sibling(core, d, s, h):
        line = (b + (NL - s, s)[d]) % NL
        ref = piece(core, line, h)
        return remote(ref, ref, fs.at[d, s, h], fr.at[d, s, h], sibling, t)

    def from_sibling(core, d, s, h):
        ref = piece(1 - core, (a + (NL - s, s)[d]) % NL, h)
        return remote(ref, ref, fs.at[d, s, h], fr.at[d, s, h], sibling, t)

    steps = [(0, 0, 0), (1, 0, 1), (0, 0, 1), (1, 0, 0)]
    for s in range(1, 4):
        steps += [(0, s, 0), (1, s, 1), (0, s, 1), (1, s, 0)]
    steps += [(0, 4, 0), (1, 4, 1)]
    sent = [p for p in steps if p[1] < 3 or (p[1] == 3 and p[0] == p[2])]
    shared = [p for p in steps if p[1] > 0 or p[0] == p[2]]

    def take(part):
        def body(core):
            if part[1] > 0:
                arrival(core, *part).wait_recv()
            if part in sent:
                ring(core, *part).start()
            if part in shared:
                to_sibling(core, *part).start()

        each_core(body)

    for part in steps[:4]:
        take(part)

    x_copies[0].wait_recv()
    fwd0 = remote(X.at[left, 0], X.at[left, 0], xfs.at[0], xfr.at[0], g, right)
    fwd0.start()
    x_copies[1].wait_recv()
    fwd1 = remote(X.at[right, 1], X.at[right, 1], xfs.at[1], xfr.at[1], g, left)
    fwd1.start()

    for part in steps[4:8]:
        take(part)

    def value_ring(d, s):
        line = (b + (NL - s, s)[d]) % NL
        return remote(
            V.at[line], V.at[line], vs.at[d, s], vr.at[d, s], second((b + (1, NL - 1)[d]) % NL), t
        )

    def value_arrival(d, s):
        line = (b + (NL - s, s)[d]) % NL
        return remote(
            V.at[line], V.at[line], vs.at[d, s - 1], vr.at[d, s - 1],
            second((b + (1, NL - 1)[d]) % NL), t,
        )

    def value_share(d, s):
        line = (z + (NL - s, s)[d]) % NL
        return remote(V.at[line], V.at[line], gs.at[d, s], gr.at[d, s], sibling, t)

    value_steps = [(0, 0), (1, 0), (0, 1), (1, 1), (0, 2), (1, 2), (0, 3), (1, 3), (0, 4)]
    value_sent = [p for p in value_steps if p[1] < (4, 3)[p[0]]]
    value_shared = [p for p in value_steps if p != (1, 0)]

    def take_value(part):
        @pl.when(c == 0)
        def _():
            if part[1] > 0:
                value_arrival(*part).wait_recv()
            if part in value_sent:
                value_ring(*part).start()
            if part in value_shared:
                value_share(*part).start()

    for part in steps[8:12]:
        take(part)

    @pl.when(c == 0)
    def _():
        for k in range(1, NL):
            remote(
                V.at[z, y], V.at[z, y], v1s.at[k], v1r.at[k], first((a + k) % NL), t
            ).wait_recv()

    take_value((0, 0))
    take_value((1, 0))

    x_copies[2].wait_recv()
    x_copies[3].wait_recv()
    fwd0.wait_recv()
    fwd1.wait_recv()
    for h in range(2):

        def norm_rows(i, carry, h=h):
            rows = pl.ds(pl.multiple_of(i * 16, 16), 16)
            total = jnp.zeros((16, 1), F32)
            for s in range(NT):
                wide = X[s, h, rows, :].astype(F32)
                total = total + jnp.sum(wide * wide, axis=1, keepdims=True)
            scale = lax.rsqrt(total / (NT * SLICE) + epsilon)
            out_rows = pl.ds(pl.multiple_of(h * BLK + i * 16, 16), 16)
            for s in range(NT):
                wide = X[s, h, rows, :].astype(F32)
                part = gain[:, s * SLICE : (s + 1) * SLICE]
                N[out_rows, s * SLICE : (s + 1) * SLICE] = (wide * scale * part).astype(BF16)
            return carry

        lax.fori_loop(0, BLK // 16, norm_rows, 0)

    for part in steps[12:]:
        take(part)

    take_value((0, 1))
    take_value((1, 1))

    for part in shared:
        each_core(lambda core, part=part: from_sibling(core, *part).wait_recv())

    for stream in range(2):

        def project(i, carry, stream=stream):
            features = pl.ds(pl.multiple_of(i * 2 * LINE, 2 * LINE), 2 * LINE)
            piece_w = W[stream, pl.ds(2 * i, 2)].reshape(2 * LINE, SW)
            prod = jnp.dot(N[:, features], piece_w, preferred_element_type=F32)
            qkv[stream] = jnp.where(i == 0, prod, qkv[stream] + prod)
            return carry

        qkv[stream] = jnp.zeros((GEN_BLK * BLK, SW), F32)
        lax.fori_loop(0, NL // 2, project, 0)

    take_value((0, 2))
    take_value((1, 2))

    tab_copy.wait_recv()
    info = []
    for block in range(GEN_BLK):
        flag, segment, place = held(block)
        there = tab_in[block : block + 1, :]
        info.append((
            flag + there,
            there,
            segment + tab_in[GEN_BLK + block : GEN_BLK + block + 1, :],
            place + tab_in[2 * GEN_BLK + block : 2 * GEN_BLK + block + 1, :],
        ))
    q_in = lax.broadcasted_iota(jnp.int32, (BLK, BLK), 0)
    k_in = lax.broadcasted_iota(jnp.int32, (BLK, BLK), 1)
    for i in range(GEN_BLK):
        for j in range(GEN_BLK):
            fi, li, si, pi = info[i]
            fj, lj, sj, pj = info[j]
            both = (fi > 0) & (fj > 0) & (li == lj) & (si == sj)
            meet = jnp.broadcast_to(jnp.where(both, 1, 0), (BLK, BLK))
            ordered = (pi * BLK + q_in) >= (pj * BLK + k_in)
            allow[i * BLK : (i + 1) * BLK, j * BLK : (j + 1) * BLK] = jnp.where(ordered, meet, 0)

    keys = qkv[0, :, 2 * HD :].astype(BF16)
    may = allow[...] > 0
    total = jnp.zeros((GEN_BLK * BLK, HD), F32)
    for head in range(HEADS):
        stream, at = (0, head) if head < 2 else (1, head - 2)
        queries = qkv[stream, :, at * HD : (at + 1) * HD].astype(BF16)
        scores = lax.dot_general(
            queries, keys, (((1,), (1,)), ((), ())), preferred_element_type=F32
        ) * HD ** (-0.5)
        masked = jnp.where(may, scores, -1e30)
        row_max = jnp.max(masked, axis=1, keepdims=True)
        raised = jnp.where(may, jnp.exp(masked - row_max), 0.0)
        denom = jnp.sum(raised, axis=1, keepdims=True)
        denom = jnp.where(denom == 0.0, 1.0, denom)
        prob = (raised / denom).astype(BF16)
        probs[head] = prob
        total = total + lax.dot_general(
            prob, cot[:, head * HD : (head + 1) * HD], (((0,), (0,)), ((), ())),
            preferred_element_type=F32,
        )
    vc[...] = total.astype(BF16)

    take_value((0, 3))
    take_value((1, 3))

    def terms(i, carry):
        features = pl.ds(pl.multiple_of(i * LINE, LINE), LINE)
        prod = lax.dot_general(
            N[:, features], vc[...], (((0,), (0,)), ((), ())), preferred_element_type=F32
        ).reshape(NL, CHIP, HD)
        R[0, :, pl.ds(pl.multiple_of(i * PART, PART), PART), :] = prod[:, :PART, :]
        R[1, i] = prod[:, PART:, :].reshape(NL * PART, HD)
        return carry

    lax.fori_loop(0, NL, terms, 0)
    Rb[...] = R[1 - c].astype(BF16)
    sum_copy = remote(Rb, SR, ss, sr, sibling, t)
    sum_copy.start()
    take_value((0, 4))
    sum_copy.wait_recv()
    for line in range(NL):
        both_cores = R[c, line] + SR[line].astype(F32)
        R[c, line] = both_cores
        H[line] = both_cores.astype(BF16)
    sums = []
    for k in (4, 3, 5, 2, 6, 1, 7):
        copy = remote(H.at[(a + k) % NL], P1.at[k], q1s.at[k], q1r.at[k], first((a + k) % NL), t)
        copy.start()
        sums.append(copy)

    @pl.when(c == 1)
    def _():
        for part in value_shared:
            value_share(*part).wait_recv()

    values = jnp.zeros((GEN_BLK * BLK, HD), F32)
    for i in range(NL):
        values = values + jnp.dot(
            N[:, i * LINE : (i + 1) * LINE], V[i].reshape(LINE, HD), preferred_element_type=F32
        )
    values = values.astype(BF16)
    for head in range(HEADS):
        att[:, head * HD : (head + 1) * HD] = jnp.dot(
            probs[head], values, preferred_element_type=F32
        ).astype(BF16)

    for copy in sums:
        copy.wait_recv()
    acc = R[c, a]
    for k in range(1, NL):
        acc = acc + P1[k].astype(F32)
    F[...] = acc.reshape(NL, PART, HD)
    last = []
    for k in (4, 3, 5, 2, 6, 1, 7):
        copy = remote(F.at[(b + k) % NL], P2.at[k], q2s.at[k], q2r.at[k], second((b + k) % NL), t)
        copy.start()
        last.append(copy)
    for copy in last:
        copy.wait_recv()
    out = F[b]
    for k in range(1, NL):
        out = out + P2[k]
    grad[...] = out

    sib_copy.wait_send()
    tab_copy.wait_send()
    fwd0.wait_send()
    fwd1.wait_send()
    sum_copy.wait_send()
    for copy in x_copies + p1 + sums + last:
        copy.wait_send()

    def all_left(core):
        for part in sent:
            ring(core, *part).wait_send()
        for part in shared:
            to_sibling(core, *part).wait_send()
        if core == 0:
            for k in range(1, NL):
                remote(
                    V.at[z, y], V.at[z, y], v1s.at[k], v1r.at[k], first((a + k) % NL), t
                ).wait_send()
            for part in value_sent:
                value_ring(*part).wait_send()
            for part in value_shared:
                value_share(*part).wait_send()

    each_core(all_left)


def shards(hidden_rows, cotangent, norm_gain, query_weight, key_weight, value_weight, source, segment, position):
    rows = GEN_BLK * BLK
    vmem = pl.BlockSpec(memory_space=pltpu.VMEM)
    smem = pl.BlockSpec(memory_space=pltpu.SMEM)
    dma = pltpu.SemaphoreType.DMA
    return pl.pallas_call(
        kernel,
        out_shape=(
            jax.ShapeDtypeStruct((rows, HEADS * HD), BF16),
            jax.ShapeDtypeStruct((PART, HD), F32),
        ),
        in_specs=[vmem] * 6 + [smem] * 3,
        out_specs=(vmem, vmem),
        scratch_shapes=[
            pltpu.VMEM((2, NL, NL, CHIP, SW), BF16),
            pltpu.VMEM((NL, NL, CHIP, HD), BF16),
            pltpu.VMEM((NT, GEN_BLK, BLK, SLICE), BF16),
            pltpu.VMEM((rows, NT * SLICE), BF16),
            pltpu.VMEM((PART, SW + HD), F32),
            pltpu.VMEM((PART, SW + HD), F32),
            pltpu.VMEM((8, 128), jnp.int32),
            pltpu.VMEM((8, 128), jnp.int32),
            pltpu.VMEM((2, rows, SW), F32),
            pltpu.VMEM((HEADS, rows, rows), BF16),
            pltpu.VMEM((rows, rows), jnp.int32),
            pltpu.VMEM((rows, HD), BF16),
            pltpu.VMEM((2, NL, NL * PART, HD), F32),
            pltpu.VMEM((NL, NL * PART, HD), BF16),
            pltpu.VMEM((NL, NL * PART, HD), BF16),
            pltpu.VMEM((NL, NL * PART, HD), BF16),
            pltpu.VMEM((NL, NL * PART, HD), BF16),
            pltpu.VMEM((NL, PART, HD), F32),
            pltpu.VMEM((NL, PART, HD), F32),
            dma, dma, dma, dma,
            dma((2, 2)), dma((2, 2)), dma((2,)), dma((2,)),
            dma((NL,)), dma((NL,)), dma((NL,)), dma((NL,)),
            dma((2, 4, 2)), dma((2, 4, 2)),
            dma((2, 4)), dma((2, 4)),
            dma((2, 5, 2)), dma((2, 5, 2)),
            dma((2, 5)), dma((2, 5)),
            dma, dma,
            dma((NL,)), dma((NL,)), dma((NL,)), dma((NL,)),
        ],
        compiler_params=pltpu.CompilerParams(
            collective_id=0, has_side_effects=True, vmem_limit_bytes=48 * 1024 * 1024
        ),
    )(
        hidden_rows, cotangent, norm_gain.reshape(1, -1), query_weight, key_weight, value_weight,
        source, segment, position,
    )


def solution(mesh):
    return jax.shard_map(
        shards,
        mesh=mesh,
        in_specs=(
            P("fsdp", "tp"),
            P("fsdp", "tp"),
            P(),
            P("fsdp", "tp"),
            P("fsdp", "tp"),
            P("fsdp", "tp"),
            P("fsdp"),
            P("fsdp"),
            P("fsdp"),
        ),
        out_specs=(P("fsdp", "tp"), P("fsdp", "tp")),
        check_vma=False,
    )
```

```python
import functools

import jax
import jax.numpy as jnp
from jax import lax
from jax.experimental import pallas as pl
from jax.experimental.pallas import tpu as pltpu
from jax.sharding import PartitionSpec as P

HD = 128
BLK = 128
GEN_BLK = 2
CAP_BLK = 4
NT_X = 4
NL = 8
NF = 128
CHIP = 80
PART = 40
LINE = NL * CHIP
SLICE = 1280
HEADS = 5
SW = 384
MESH = pl.DeviceIdType.MESH
F32 = jnp.float32
BF16 = jnp.bfloat16

epsilon = 1e-06


def kernel(
    hid, cot_in, gain_in, wq_in, wk_in, wv_in, src_in, seg_in, pos_in,
    att, grad,
    cot, gain, wq, wk, wv, src, seg, pos,
    W, V, X, NT, stage, sib, tab_out, tab_in, qkv, probs, allow, vc, sq_out, sq_in, scale,
    R, Rb, SR, H, M, P1, F, P2,
    ld, sib_s, sib_r, tab_s, tab_r, xs, xr, xfs, xfr,
    sqs, sqr, p1s, p1r, v1s, v1r, os, rs, rr, vs, vr, fs, fr, f4s, f4r, gs, gr,
    ss, sr, ms, mr, q1s, q1r, q2s, q2r,
):
    g = lax.axis_index("fsdp")
    t = lax.axis_index("tp")
    c = g % 2
    y = (g // 2) % NL
    z = g // (2 * NL)
    a = y + c * (z - y)
    b = z + c * (y - z)

    def first(i):
        return ((z + c * (i - z)) * NL + (i + c * (y - i))) * 2 + c

    def second(i):
        return ((i + c * (z - i)) * NL + (y + c * (i - y))) * 2 + c

    sibling = g + 1 - 2 * c
    before = (g + NF - 1) % NF
    other = (g + NF - 1 + 2 * c) % NF
    right, left, across = (t + 1) % NT_X, (t + NT_X - 1) % NT_X, (t + 2) % NT_X

    barrier = pltpu.get_barrier_semaphore()

    def greet(f, s):
        pl.semaphore_signal(barrier, inc=1, device_id=(f, s), device_id_type=MESH)

    greet(sibling, t)
    greet(other, t)
    for s in (right, left, across):
        greet(g, s)
    for k in (1, 2, NL - 2, NL - 1):
        greet(first((a + k) % NL), t)
    for k in (1, NL - 1):
        greet(second((b + k) % NL), t)

    def remote(source, target, send, recv, f, s):
        return pltpu.make_async_remote_copy(
            src_ref=source, dst_ref=target, send_sem=send, recv_sem=recv,
            device_id=(f, s), device_id_type=MESH,
        )

    loads = {}
    for i, (name, source, target) in enumerate((
        ("wq", wq_in, wq), ("wk", wk_in, wk), ("wv", wv_in, wv),
        ("src", src_in, src), ("seg", seg_in, seg), ("pos", pos_in, pos),
        ("gain", gain_in, gain),
        ("x0", hid.at[pl.ds(0, BLK)], X.at[t, 0]), ("x1", hid.at[pl.ds(BLK, BLK)], X.at[t, 1]),
        ("cot", cot_in, cot),
    )):
        loads[name] = pltpu.make_async_copy(source, target, ld.at[i])
        loads[name].start()

    for name in ("wq", "wk", "wv"):
        loads[name].wait()
    stream0 = jnp.concatenate([wq[:, : 2 * HD].astype(F32), wk[...].astype(F32)], axis=1)
    stream1 = wq[:, 2 * HD :].astype(F32)
    value_rows = wv[...].astype(F32)
    stage[:, :SW] = jnp.where(c == 0, stream1, stream0)
    stage[:, SW:] = value_rows

    for name in ("src", "seg", "pos"):
        loads[name].wait()

    def held(block):
        flag = jnp.int32(0)
        segment = jnp.int32(0)
        place = jnp.int32(0)
        for s in range(CAP_BLK):
            hit = src[s] == block
            flag = flag + jnp.where(hit, 1, 0)
            segment = segment + jnp.where(hit, seg[s], 0)
            place = place + jnp.where(hit, pos[s], 0)
        return flag, segment, place

    row = lax.broadcasted_iota(jnp.int32, (8, 128), 0)
    table = jnp.zeros((8, 128), jnp.int32)
    for block in range(GEN_BLK):
        for item, value in enumerate(held(GEN_BLK + block)):
            table = jnp.where(row == GEN_BLK * item + block, value, table)
    tab_out[...] = table

    for name in ("x0", "x1"):
        loads[name].wait()
    squares = jnp.zeros((GEN_BLK * BLK, 128), F32)
    for j in range(SLICE // 128):
        wide = X[t, :, :, j * 128 : (j + 1) * 128].reshape(GEN_BLK * BLK, 128).astype(F32)
        squares = squares + wide * wide
    own_squares = jnp.sum(squares.T, axis=0, keepdims=True)
    sq_out[...] = jnp.broadcast_to(own_squares, (8, GEN_BLK * BLK))

    pl.semaphore_wait(barrier, 11)

    sib_copy = remote(stage, sib, sib_s, sib_r, sibling, t)
    sib_copy.start()
    sq_copies = [
        remote(sq_out, sq_in.at[i], sqs.at[i], sqr.at[i], g, s)
        for i, s in enumerate((right, left, across))
    ]
    for copy in sq_copies:
        copy.start()
    x_copies = []
    for d, h in ((0, 0), (1, 1), (0, 1), (1, 0)):
        copy = remote(
            hid.at[pl.ds(BLK * h, BLK)], X.at[t, h], xs.at[d, h], xr.at[d, h], g, (right, left)[d]
        )
        copy.start()
        x_copies.append(copy)
    tab_copy = remote(tab_out, tab_in, tab_s, tab_r, before, t)
    tab_copy.start()

    sib_copy.wait_recv()
    mine = jnp.where(c == 0, stream0, stream1)
    theirs = sib[:, :SW]
    top = jnp.where(c == 0, mine, theirs)
    bottom = jnp.where(c == 0, theirs, mine)
    W[c, z, y] = jnp.concatenate([top, bottom], axis=0).astype(BF16)

    def each_core(body):
        for core in range(2):

            @pl.when(c == core)
            def _(core=core):
                body(core)

    def block_ref(item):
        return W.at[c, z + c * (item - z), item + c * (y - item)]

    def along(i):
        whose, to = ((0, 1), (0, 7), (0, 2), (0, 6), (7, 2), (1, 6), (6, 2))[i]
        ref = block_ref((a + whose) % NL)
        return remote(ref, ref, p1s.at[i], p1r.at[i], first((a + to) % NL), t)

    got = (7, 1, 6, 2, 5, 3, 4)

    def along_arrival(i):
        ref = block_ref((a + got[i]) % NL)
        return remote(ref, ref, p1s.at[i], p1r.at[i], first((a + got[i]) % NL), t)

    def own_line(k, d):
        item = (a + k) % NL
        ref = block_ref(item)
        return remote(
            ref, ref, os.at[d, k], rr.at[d, 0, (item // 2 + 4 - a // 2) % 4],
            second((b + (1, NL - 1)[d]) % NL), t,
        )

    def take_block(i):
        along_arrival(i).wait_recv()
        if i < 3:
            along(4 + i).start()
        own_line(got[i], 0).start()
        own_line(got[i], 1).start()

    for i in range(4):
        along(i).start()
    own_line(0, 0).start()
    own_line(0, 1).start()
    for i in range(4):
        take_block(i)

    def piece(core, line, j):
        items = pl.ds(2 * ((a // 2 + j) % 4), 2)
        return W.at[0, line, items] if core == 0 else W.at[1, items, line]

    def whole(core, line):
        return W.at[0, line] if core == 0 else W.at[1, :, line]

    def ring(core, d, s, j):
        ref = piece(core, (b + (NL - s, s)[d]) % NL, j)
        target = second((b + (1, NL - 1)[d]) % NL)
        return remote(ref, ref, rs.at[d, s, j], rr.at[d, s, j], target, t)

    def arrival(core, d, s, j):
        ref = piece(core, (b + (NL - s, s)[d]) % NL, j)
        target = second((b + (1, NL - 1)[d]) % NL)
        return remote(ref, ref, rs.at[d, s - 1, j], rr.at[d, s - 1, j], target, t)

    def to_sibling(core, d, s):
        ref = whole(core, (b + (NL - s, s)[d]) % NL)
        return remote(ref, ref, fs.at[d, s], fr.at[d, s], sibling, t)

    def from_sibling(core, d, s):
        ref = whole(1 - core, (a + (NL - s, s)[d]) % NL)
        return remote(ref, ref, fs.at[d, s], fr.at[d, s], sibling, t)

    def last_to_sibling(core, j):
        ref = piece(core, (b + 4) % NL, j)
        return remote(ref, ref, f4s.at[j], f4r.at[j], sibling, t)

    def last_from_sibling(core, j):
        items = pl.ds(2 * ((b // 2 + j) % 4), 2)
        line = (a + 4) % NL
        ref = W.at[0, line, items] if core == 1 else W.at[1, items, line]
        return remote(ref, ref, f4s.at[j], f4r.at[j], sibling, t)

    order = (0, 1, 3, 2)
    steps = [(d, s, j) for s in range(1, 4) for j in order for d in range(2)]
    last_steps = [(0, 4, 0), (1, 4, 3), (0, 4, 1), (1, 4, 2)]
    sent = [p for p in steps if p[1] < 3 or p[2] in ((0, 1), (3, 2))[p[0]]]

    def take(s, js):
        def body(core):
            for part in steps + last_steps:
                if part[1] == s and part[2] in js:
                    arrival(core, *part).wait_recv()
                    if part in sent:
                        ring(core, *part).start()
                    if s == 4:
                        last_to_sibling(core, part[2]).start()

        each_core(body)

    def share(s):
        each_core(lambda core: [to_sibling(core, d, s).start() for d in range(min(s + 1, 2))])

    def from_other(s):
        def body(core):
            if s == 4:
                for j in order:
                    last_from_sibling(core, j).wait_recv()
            else:
                for d in range(min(s + 1, 2)):
                    from_sibling(core, d, s).wait_recv()

        each_core(body)

    take(1, (0,))
    for i in range(4, 7):
        take_block(i)
    share(0)

    top = jnp.where(c == 0, value_rows, sib[:, SW:])
    bottom = jnp.where(c == 0, sib[:, SW:], value_rows)

    def value_first(k):
        return remote(
            V.at[z, y], V.at[z, y], v1s.at[k], v1r.at[k], first((a + k) % NL), t
        )

    @pl.when(c == 0)
    def _():
        V[z, y] = jnp.concatenate([top, bottom], axis=0).astype(BF16)
        for k in (1, 7, 2, 6, 3, 5, 4):
            value_first(k).start()

    x_copies[0].wait_recv()
    fwd0 = remote(X.at[left, 0], X.at[left, 0], xfs.at[0], xfr.at[0], g, right)
    fwd0.start()
    x_copies[1].wait_recv()
    fwd1 = remote(X.at[right, 1], X.at[right, 1], xfs.at[1], xfr.at[1], g, left)
    fwd1.start()

    total = own_squares
    for i, copy in enumerate(sq_copies):
        copy.wait_recv()
        total = total + sq_in[i, :1, :]
    by_token = lax.rsqrt(total / (NT_X * SLICE) + epsilon)
    scale[...] = jnp.broadcast_to(by_token, (128, GEN_BLK * BLK)).T

    def prepare(s):
        def half_slice(i, carry):
            blocks = []
            for j in range(5):
                columns = pl.ds(pl.multiple_of(i * LINE + j * 128, 128), 128)
                wide = X[s, :, :, columns].reshape(GEN_BLK * BLK, 128).astype(F32)
                blocks.append((wide * scale[...] * gain[s, :, columns]).astype(BF16).T)
            NT[2 * s + i] = jnp.concatenate(blocks, axis=0).reshape(NL, CHIP, GEN_BLK * BLK)
            return carry

        lax.fori_loop(0, 2, half_slice, 0)

    loads["gain"].wait()
    take(1, (1,))
    prepare(t)
    take(1, (3, 2))
    share(1)
    take(2, (0, 1, 3))
    x_copies[2].wait_recv()
    x_copies[3].wait_recv()
    prepare(left)
    take(2, (2,))
    share(2)
    prepare(right)
    take(3, (0, 1, 3, 2))
    share(3)

    def value_ring(d, s):
        line = (b + (NL - s, s)[d]) % NL
        return remote(
            V.at[line], V.at[line], vs.at[d, s], vr.at[d, s], second((b + (1, NL - 1)[d]) % NL), t
        )

    def value_arrival(d, s):
        line = (b + (NL - s, s)[d]) % NL
        return remote(
            V.at[line], V.at[line], vs.at[d, s - 1], vr.at[d, s - 1],
            second((b + (1, NL - 1)[d]) % NL), t,
        )

    def value_share(d, s):
        line = (z + (NL - s, s)[d]) % NL
        return remote(V.at[line], V.at[line], gs.at[d, s], gr.at[d, s], sibling, t)

    value_steps = [(0, 0), (1, 0), (0, 1), (1, 1), (0, 2), (1, 2), (0, 3), (1, 3), (0, 4)]
    value_sent = [p for p in value_steps if p[1] < (4, 3)[p[0]]]
    value_shared = [p for p in value_steps if p != (1, 0)]

    def take_value(s):
        @pl.when(c == 0)
        def _():
            for part in value_steps:
                if part[1] == s:
                    if s > 0:
                        value_arrival(*part).wait_recv()
                    if part in value_sent:
                        value_ring(*part).start()
                    if part in value_shared:
                        value_share(*part).start()

    @pl.when(c == 0)
    def _():
        for k in range(1, NL):
            value_first(k).wait_recv()

    take_value(0)
    fwd0.wait_recv()
    fwd1.wait_recv()
    prepare(across)

    def project(one, two, fresh):
        for stream in range(2):
            def pick(ref, line, stream=stream):
                return ref[line] if stream == 0 else ref[:, line]

            at = (z, y)[stream]
            l0, l1 = (at + one) % NL, (at + two) % NL
            rows = jnp.concatenate(
                [pick(NT, l0).reshape(LINE, -1), pick(NT, l1).reshape(LINE, -1)], axis=0
            )
            weights = jnp.concatenate(
                [pick(W.at[stream], l0).reshape(LINE, -1), pick(W.at[stream], l1).reshape(LINE, -1)],
                axis=0,
            )
            prod = lax.dot_general(
                rows, weights, (((0,), (0,)), ((), ())), preferred_element_type=F32
            )
            qkv[stream] = prod if fresh else qkv[stream] + prod

    from_other(0)
    from_other(1)
    project(1, 7, True)
    from_other(2)
    project(2, 6, False)
    take(4, order)
    from_other(3)
    project(3, 5, False)

    tab_copy.wait_recv()
    info = []
    for block in range(GEN_BLK):
        flag, segment, place = held(block)
        there = tab_in[block : block + 1, :]
        info.append((
            flag + there,
            there,
            segment + tab_in[GEN_BLK + block : GEN_BLK + block + 1, :],
            place + tab_in[2 * GEN_BLK + block : 2 * GEN_BLK + block + 1, :],
        ))
    q_in = lax.broadcasted_iota(jnp.int32, (BLK, BLK), 0)
    k_in = lax.broadcasted_iota(jnp.int32, (BLK, BLK), 1)
    for i in range(GEN_BLK):
        for j in range(GEN_BLK):
            fi, li, si, pi = info[i]
            fj, lj, sj, pj = info[j]
            both = (fi > 0) & (fj > 0) & (li == lj) & (si == sj)
            meet = jnp.broadcast_to(jnp.where(both, 1, 0), (BLK, BLK))
            ordered = (pi * BLK + q_in) >= (pj * BLK + k_in)
            allow[i * BLK : (i + 1) * BLK, j * BLK : (j + 1) * BLK] = jnp.where(ordered, meet, 0)

    take_value(1)
    from_other(4)
    project(0, 4, False)

    loads["cot"].wait()
    keys = qkv[0, :, 2 * HD :].astype(BF16)
    may = allow[...] > 0
    total = jnp.zeros((GEN_BLK * BLK, HD), F32)
    for head in range(HEADS):
        stream, at = (0, head) if head < 2 else (1, head - 2)
        queries = qkv[stream, :, at * HD : (at + 1) * HD].astype(BF16)
        scores = lax.dot_general(
            queries, keys, (((1,), (1,)), ((), ())), preferred_element_type=F32
        ) * HD ** (-0.5)
        masked = jnp.where(may, scores, -1e30)
        row_max = jnp.max(masked, axis=1, keepdims=True)
        raised = jnp.where(may, jnp.exp(masked - row_max), 0.0)
        denom = jnp.sum(raised, axis=1, keepdims=True)
        denom = jnp.where(denom == 0.0, 1.0, denom)
        prob = (raised / denom).astype(BF16)
        probs[head] = prob
        total = total + lax.dot_general(
            prob, cot[:, head * HD : (head + 1) * HD], (((0,), (0,)), ((), ())),
            preferred_element_type=F32,
        )
    vc[...] = total.astype(BF16)
    take_value(2)

    def sum_copy(i):
        return remote(Rb.at[i], SR.at[i], ss.at[i], sr.at[i], sibling, t)

    def terms(i, carry):
        rows = jnp.concatenate(
            [NT[i + c * (m - i), m + c * (i - m)] for m in range(NL)], axis=0
        )
        prod = jnp.dot(rows, vc[...], preferred_element_type=F32).reshape(NL, CHIP, HD)
        top, bottom = prod[:, :PART, :], prod[:, PART:, :]
        Rb[i] = jnp.where(c == 0, bottom, top).reshape(NL * PART, HD).astype(BF16)
        sum_copy(i).start()
        R[:, pl.ds(pl.multiple_of(i * PART, 8), PART), :] = jnp.where(c == 0, top, bottom)
        return carry

    lax.fori_loop(0, NL, terms, 0)

    def both_cores(k):
        line = (a + k) % NL
        sum_copy(line).wait_recv()
        return R[line] + SR[line].astype(F32)

    H[4] = both_cores(4).astype(BF16)
    merge = remote(H.at[4], M, ms, mr, first((a + NL - 1) % NL), t)
    merge.start()
    sums = []
    for k in (3, 2, 6, 5, 1, 7):
        value = both_cores(k)
        if k == 5:
            merge.wait_recv()
            value = value + M[...].astype(F32)
        H[k] = value.astype(BF16)
        copy = remote(H.at[k], P1.at[k], q1s.at[k], q1r.at[k], first((a + k) % NL), t)
        copy.start()
        sums.append(copy)
    acc = both_cores(0)

    take_value(3)
    for copy in sums:
        copy.wait_recv()
    for k in (1, 2, 3, 5, 6, 7):
        acc = acc + P1[k].astype(F32)
    F[...] = acc.reshape(NL, PART, HD)
    last = []
    for k in (4, 3, 5, 2, 6, 1, 7):
        copy = remote(F.at[(b + k) % NL], P2.at[k], q2s.at[k], q2r.at[k], second((b + k) % NL), t)
        copy.start()
        last.append(copy)
    take_value(4)

    @pl.when(c == 1)
    def _():
        for part in value_shared:
            value_share(*part).wait_recv()

    values = jnp.zeros((GEN_BLK * BLK, HD), F32)
    for i in range(NL):
        values = values + lax.dot_general(
            NT[i].reshape(LINE, -1), V[i].reshape(LINE, HD), (((0,), (0,)), ((), ())),
            preferred_element_type=F32,
        )
    values = values.astype(BF16)
    for head in range(HEADS):
        att[:, head * HD : (head + 1) * HD] = jnp.dot(
            probs[head], values, preferred_element_type=F32
        ).astype(BF16)

    for copy in last:
        copy.wait_recv()
    out = F[b]
    for k in range(1, NL):
        out = out + P2[k]
    grad[...] = out

    for copy in x_copies + sq_copies + sums + last + [sib_copy, tab_copy, fwd0, fwd1, merge]:
        copy.wait_send()
    for i in range(NL):
        sum_copy(i).wait_send()
    for i in range(7):
        along(i).wait_send()
    for k in range(NL):
        own_line(k, 0).wait_send()
        own_line(k, 1).wait_send()

    def all_left(core):
        for part in sent:
            ring(core, *part).wait_send()
        for s in range(4):
            for d in range(min(s + 1, 2)):
                to_sibling(core, d, s).wait_send()
        for j in order:
            last_to_sibling(core, j).wait_send()
        if core == 0:
            for k in range(1, NL):
                value_first(k).wait_send()
            for part in value_sent:
                value_ring(*part).wait_send()
            for part in value_shared:
                value_share(*part).wait_send()

    each_core(all_left)


def shards(hidden_rows, cotangent, norm_gain, query_weight, key_weight, value_weight, source, segment, position):
    rows = GEN_BLK * BLK
    vmem = pl.BlockSpec(memory_space=pltpu.VMEM)
    dma = pltpu.SemaphoreType.DMA
    return pl.pallas_call(
        kernel,
        out_shape=(
            jax.ShapeDtypeStruct((rows, HEADS * HD), BF16),
            jax.ShapeDtypeStruct((PART, HD), F32),
        ),
        in_specs=[pl.BlockSpec(memory_space=pltpu.HBM)] * 9,
        out_specs=(vmem, vmem),
        scratch_shapes=[
            pltpu.VMEM((rows, HEADS * HD), BF16),
            pltpu.VMEM((NT_X, 1, SLICE), F32),
            pltpu.VMEM((PART, HEADS * HD), BF16),
            pltpu.VMEM((PART, HD), BF16),
            pltpu.VMEM((PART, HD), BF16),
            pltpu.SMEM((CAP_BLK,), jnp.int32),
            pltpu.SMEM((CAP_BLK,), jnp.int32),
            pltpu.SMEM((CAP_BLK,), jnp.int32),
            pltpu.VMEM((2, NL, NL, CHIP, SW), BF16),
            pltpu.VMEM((NL, NL, CHIP, HD), BF16),
            pltpu.VMEM((NT_X, GEN_BLK, BLK, SLICE), BF16),
            pltpu.VMEM((NL, NL, CHIP, rows), BF16),
            pltpu.VMEM((PART, SW + HD), F32),
            pltpu.VMEM((PART, SW + HD), F32),
            pltpu.VMEM((8, 128), jnp.int32),
            pltpu.VMEM((8, 128), jnp.int32),
            pltpu.VMEM((2, rows, SW), F32),
            pltpu.VMEM((HEADS, rows, rows), BF16),
            pltpu.VMEM((rows, rows), jnp.int32),
            pltpu.VMEM((rows, HD), BF16),
            pltpu.VMEM((8, rows), F32),
            pltpu.VMEM((3, 8, rows), F32),
            pltpu.VMEM((rows, HD), F32),
            pltpu.VMEM((NL, NL * PART, HD), F32),
            pltpu.VMEM((NL, NL * PART, HD), BF16),
            pltpu.VMEM((NL, NL * PART, HD), BF16),
            pltpu.VMEM((NL, NL * PART, HD), BF16),
            pltpu.VMEM((NL * PART, HD), BF16),
            pltpu.VMEM((NL, NL * PART, HD), BF16),
            pltpu.VMEM((NL, PART, HD), F32),
            pltpu.VMEM((NL, PART, HD), F32),
            dma((10,)),
            dma, dma, dma, dma,
            dma((2, 2)), dma((2, 2)), dma((2,)), dma((2,)),
            dma((3,)), dma((3,)),
            dma((7,)), dma((7,)),
            dma((NL,)), dma((NL,)),
            dma((2, NL)),
            dma((2, 4, 4)), dma((2, 4, 4)),
            dma((2, 4)), dma((2, 4)),
            dma((2, 4)), dma((2, 4)), dma((4,)), dma((4,)),
            dma((2, 5)), dma((2, 5)),
            dma((NL,)), dma((NL,)),
            dma, dma,
            dma((NL,)), dma((NL,)), dma((NL,)), dma((NL,)),
        ],
        compiler_params=pltpu.CompilerParams(
            collective_id=0, has_side_effects=True, vmem_limit_bytes=60 * 1024 * 1024
        ),
    )(
        hidden_rows, cotangent, norm_gain.reshape(NT_X, 1, SLICE), query_weight, key_weight, value_weight,
        source, segment, position,
    )


def solution(mesh):
    return jax.shard_map(
        shards,
        mesh=mesh,
        in_specs=(
            P("fsdp", "tp"),
            P("fsdp", "tp"),
            P(),
            P("fsdp", "tp"),
            P("fsdp", "tp"),
            P("fsdp", "tp"),
            P("fsdp"),
            P("fsdp"),
            P("fsdp"),
        ),
        out_specs=(P("fsdp", "tp"), P("fsdp", "tp")),
        check_vma=False,
    )
```

```python
import functools

import jax
import jax.numpy as jnp
from jax import lax
from jax.experimental import pallas as pl
from jax.experimental.pallas import tpu as pltpu
from jax.sharding import PartitionSpec as P

HD = 128
BLK = 128
GEN_BLK = 2
CAP_BLK = 4
NT_X = 4
NL = 8
NF = 128
CHIP = 80
PART = 40
LINE = NL * CHIP
SLICE = 1280
HEADS = 5
SW = 384
MESH = pl.DeviceIdType.MESH
F32 = jnp.float32
BF16 = jnp.bfloat16

epsilon = 1e-06


def kernel(
    hid, cot_in, gain_in, wq_in, wk_in, wv_in, src_in, seg_in, pos_in,
    att, grad,
    cot, gain, wq, wk, wv, src, seg, pos,
    W, V, X, NT, stage, sib, tab_out, tab_in, qkv, probs, allow, vc, sq_out, sq_in, scale,
    TH, TH_in, top_rows, vc_in, R, H, M, P1, F, P2,
    ld, sib_s, sib_r, tab_s, tab_r, xs, xr, xfs, xfr,
    sqs, sqr, p1s, p1r, v1s, v1r, os, rs, rr, vs, vr, fs, fr, f4s, f4r, gs, gr,
    ths, thr, vcs, vcr, ms, mr, q1s, q1r, q2s, q2r,
):
    g = lax.axis_index("fsdp")
    t = lax.axis_index("tp")
    c = g % 2
    y = (g // 2) % NL
    z = g // (2 * NL)
    a = y + c * (z - y)
    b = z + c * (y - z)

    def first(i):
        return ((z + c * (i - z)) * NL + (i + c * (y - i))) * 2 + c

    def second(i):
        return ((i + c * (z - i)) * NL + (y + c * (i - y))) * 2 + c

    sibling = g + 1 - 2 * c
    before = (g + NF - 1) % NF
    other = (g + NF - 1 + 2 * c) % NF
    right, left, across = (t + 1) % NT_X, (t + NT_X - 1) % NT_X, (t + 2) % NT_X

    barrier = pltpu.get_barrier_semaphore()

    def greet(f, s):
        pl.semaphore_signal(barrier, inc=1, device_id=(f, s), device_id_type=MESH)

    greet(sibling, t)
    greet(other, t)
    for s in (right, left, across):
        greet(g, s)
    for k in (1, 2, NL - 2, NL - 1):
        greet(first((a + k) % NL), t)
    for k in (1, NL - 1):
        greet(second((b + k) % NL), t)

    def remote(source, target, send, recv, f, s):
        return pltpu.make_async_remote_copy(
            src_ref=source, dst_ref=target, send_sem=send, recv_sem=recv,
            device_id=(f, s), device_id_type=MESH,
        )

    loads = {}
    for i, (name, source, target) in enumerate((
        ("wq", wq_in, wq), ("wk", wk_in, wk), ("wv", wv_in, wv),
        ("src", src_in, src), ("seg", seg_in, seg), ("pos", pos_in, pos),
        ("gain", gain_in, gain),
        ("x0", hid.at[pl.ds(0, BLK)], X.at[t, 0]), ("x1", hid.at[pl.ds(BLK, BLK)], X.at[t, 1]),
        ("cot", cot_in, cot),
    )):
        loads[name] = pltpu.make_async_copy(source, target, ld.at[i])
        loads[name].start()

    for name in ("wq", "wk", "wv"):
        loads[name].wait()
    stream0 = jnp.concatenate([wq[:, : 2 * HD].astype(F32), wk[...].astype(F32)], axis=1)
    stream1 = wq[:, 2 * HD :].astype(F32)
    value_rows = wv[...].astype(F32)
    stage[:, :SW] = jnp.where(c == 0, stream1, stream0)
    stage[:, SW:] = value_rows

    for name in ("src", "seg", "pos"):
        loads[name].wait()

    def held(block):
        flag = jnp.int32(0)
        segment = jnp.int32(0)
        place = jnp.int32(0)
        for s in range(CAP_BLK):
            hit = src[s] == block
            flag = flag + jnp.where(hit, 1, 0)
            segment = segment + jnp.where(hit, seg[s], 0)
            place = place + jnp.where(hit, pos[s], 0)
        return flag, segment, place

    row = lax.broadcasted_iota(jnp.int32, (8, 128), 0)
    table = jnp.zeros((8, 128), jnp.int32)
    for block in range(GEN_BLK):
        for item, value in enumerate(held(GEN_BLK + block)):
            table = jnp.where(row == GEN_BLK * item + block, value, table)
    tab_out[...] = table

    for name in ("x0", "x1"):
        loads[name].wait()
    squares = jnp.zeros((GEN_BLK * BLK, 128), F32)
    for j in range(SLICE // 128):
        wide = X[t, :, :, j * 128 : (j + 1) * 128].reshape(GEN_BLK * BLK, 128).astype(F32)
        squares = squares + wide * wide
    own_squares = jnp.sum(squares.T, axis=0, keepdims=True)
    sq_out[...] = jnp.broadcast_to(own_squares, (8, GEN_BLK * BLK))

    pl.semaphore_wait(barrier, 11)

    sib_copy = remote(stage, sib, sib_s, sib_r, sibling, t)
    sib_copy.start()
    sq_copies = [
        remote(sq_out, sq_in.at[i], sqs.at[i], sqr.at[i], g, s)
        for i, s in enumerate((right, left, across))
    ]
    for copy in sq_copies:
        copy.start()
    x_copies = []
    for d, h in ((0, 0), (1, 1), (0, 1), (1, 0)):
        copy = remote(
            hid.at[pl.ds(BLK * h, BLK)], X.at[t, h], xs.at[d, h], xr.at[d, h], g, (right, left)[d]
        )
        copy.start()
        x_copies.append(copy)
    tab_copy = remote(tab_out, tab_in, tab_s, tab_r, before, t)
    tab_copy.start()

    sib_copy.wait_recv()
    mine = jnp.where(c == 0, stream0, stream1)
    theirs = sib[:, :SW]
    top = jnp.where(c == 0, mine, theirs)
    bottom = jnp.where(c == 0, theirs, mine)
    W[c, z, y] = jnp.concatenate([top, bottom], axis=0).astype(BF16)

    def each_core(body):
        for core in range(2):

            @pl.when(c == core)
            def _(core=core):
                body(core)

    def block_ref(item):
        return W.at[c, z + c * (item - z), item + c * (y - item)]

    def along(i):
        whose, to = ((0, 1), (0, 7), (0, 2), (0, 6), (6, 1), (2, 7), (6, 2))[i]
        ref = block_ref((a + whose) % NL)
        return remote(ref, ref, p1s.at[i], p1r.at[i], first((a + to) % NL), t)

    got = (7, 1, 6, 2, 5, 3, 4)

    def along_arrival(i):
        ref = block_ref((a + got[i]) % NL)
        return remote(ref, ref, p1s.at[i], p1r.at[i], first((a + 1) % NL), t)

    def own_line(k, d):
        item = (a + k) % NL
        ref = block_ref(item)
        return remote(
            ref, ref, os.at[d, k], rr.at[d, 0, (item // 2 + 4 - a // 2) % 4],
            second((b + (1, NL - 1)[d]) % NL), t,
        )

    def take_block(i):
        along_arrival(i).wait_recv()
        for relay in ((), (), (4, 6), (5,), (), (), ())[i]:
            along(relay).start()
        own_line(got[i], 0).start()
        own_line(got[i], 1).start()

    for i in range(4):
        along(i).start()
    own_line(0, 0).start()
    own_line(0, 1).start()
    for i in range(4):
        take_block(i)

    def piece(core, line, j):
        items = pl.ds(2 * ((a // 2 + j) % 4), 2)
        return W.at[0, line, items] if core == 0 else W.at[1, items, line]

    def whole(core, line):
        return W.at[0, line] if core == 0 else W.at[1, :, line]

    def ring(core, d, s, j):
        ref = piece(core, (b + (NL - s, s)[d]) % NL, j)
        target = second((b + (1, NL - 1)[d]) % NL)
        return remote(ref, ref, rs.at[d, s, j], rr.at[d, s, j], target, t)

    def arrival(core, d, s, j):
        ref = piece(core, (b + (NL - s, s)[d]) % NL, j)
        target = second((b + (1, NL - 1)[d]) % NL)
        return remote(ref, ref, rs.at[d, s - 1, j], rr.at[d, s - 1, j], target, t)

    def to_sibling(core, d, s):
        ref = whole(core, (b + (NL - s, s)[d]) % NL)
        return remote(ref, ref, fs.at[d, s], fr.at[d, s], sibling, t)

    def from_sibling(core, d, s):
        ref = whole(1 - core, (a + (NL - s, s)[d]) % NL)
        return remote(ref, ref, fs.at[d, s], fr.at[d, s], sibling, t)

    def last_to_sibling(core, j):
        ref = piece(core, (b + 4) % NL, j)
        return remote(ref, ref, f4s.at[j], f4r.at[j], sibling, t)

    def last_from_sibling(core, j):
        items = pl.ds(2 * ((b // 2 + j) % 4), 2)
        line = (a + 4) % NL
        ref = W.at[0, line, items] if core == 1 else W.at[1, items, line]
        return remote(ref, ref, f4s.at[j], f4r.at[j], sibling, t)

    orders = ((0, 1, 3, 2), (0, 3, 2, 1))
    steps = [(d, s, orders[d][i]) for s in range(1, 4) for i in range(4) for d in range(2)]
    last_steps = [(0, 4, 0), (1, 4, 3), (0, 4, 1), (1, 4, 2)]
    sent = [p for p in steps if p[1] < 3 or p[2] in ((0, 1), (3, 2))[p[0]]]

    def take(s, places):
        def body(core):
            for part in steps + last_steps:
                if part[1] == s and orders[part[0]].index(part[2]) in places:
                    arrival(core, *part).wait_recv()
                    if part in sent:
                        ring(core, *part).start()
                    if s == 4:
                        last_to_sibling(core, part[2]).start()

        each_core(body)

    def share(s):
        each_core(lambda core: [to_sibling(core, d, s).start() for d in range(min(s + 1, 2))])

    def from_other(s):
        def body(core):
            if s == 4:
                for j in range(4):
                    last_from_sibling(core, j).wait_recv()
            else:
                for d in range(min(s + 1, 2)):
                    from_sibling(core, d, s).wait_recv()

        each_core(body)

    take(1, (0,))
    for i in range(4, 7):
        take_block(i)
    share(0)

    top = jnp.where(c == 0, value_rows, sib[:, SW:])
    bottom = jnp.where(c == 0, sib[:, SW:], value_rows)

    def value_first(k):
        return remote(
            V.at[z, y], V.at[z, y], v1s.at[k], v1r.at[k], first((a + k) % NL), t
        )

    @pl.when(c == 1)
    def _():
        V[z, y] = jnp.concatenate([top, bottom], axis=0).astype(BF16)
        for k in (1, 7, 2, 6, 3, 5, 4):
            value_first(k).start()

    x_copies[0].wait_recv()
    fwd0 = remote(X.at[left, 0], X.at[left, 0], xfs.at[0], xfr.at[0], g, right)
    fwd0.start()
    x_copies[1].wait_recv()
    fwd1 = remote(X.at[right, 1], X.at[right, 1], xfs.at[1], xfr.at[1], g, left)
    fwd1.start()

    total = own_squares
    for i, copy in enumerate(sq_copies):
        copy.wait_recv()
        total = total + sq_in[i, :1, :]
    by_token = lax.rsqrt(total / (NT_X * SLICE) + epsilon)
    scale[...] = jnp.broadcast_to(by_token, (128, GEN_BLK * BLK)).T

    def prepare(s):
        for i in range(2):
            blocks = []
            for j in range(5):
                columns = pl.ds(i * LINE + j * 128, 128)
                wide = X[s, :, :, columns].reshape(GEN_BLK * BLK, 128).astype(F32)
                blocks.append((wide * scale[...] * gain[s, :, columns]).T)
            line = jnp.concatenate(blocks, axis=0).reshape(NL, CHIP, GEN_BLK * BLK)
            NT[2 * s + i] = line.astype(BF16)
            TH[1, 2 * s + i] = line[:, PART:].reshape(NT_X, CHIP, -1).astype(BF16)
            top_rows[:, i * PART : (i + 1) * PART, :] = line[:, :PART]
        TH[0, :, s] = top_rows[...].astype(BF16)

    loads["gain"].wait()
    take(1, (1,))
    prepare(t)
    take(1, (2, 3))
    share(1)
    def value_line(at, d, s):
        return V.at[:, (at + (NL - s, s)[d]) % NL]

    def value_ring(d, s):
        ref = value_line(b, d, s)
        return remote(ref, ref, vs.at[d, s], vr.at[d, s], second((b + (1, NL - 1)[d]) % NL), t)

    def value_arrival(d, s):
        ref = value_line(b, d, s)
        return remote(
            ref, ref, vs.at[d, s - 1], vr.at[d, s - 1], second((b + (1, NL - 1)[d]) % NL), t
        )

    def value_share(d, s):
        ref = value_line(y, d, s)
        return remote(ref, ref, gs.at[d, s], gr.at[d, s], sibling, t)

    value_steps = [(0, 0), (1, 0), (0, 1), (1, 1), (0, 2), (1, 2), (0, 3), (1, 3), (0, 4)]
    value_sent = [p for p in value_steps if p[1] < (4, 3)[p[0]]]
    value_shared = [p for p in value_steps if p != (1, 0)]

    def take_value(s):
        @pl.when(c == 1)
        def _():
            for part in value_steps:
                if part[1] == s:
                    if s > 0:
                        value_arrival(*part).wait_recv()
                    if part in value_sent:
                        value_ring(*part).start()
                    if part in value_shared:
                        value_share(*part).start()

    take(2, (0, 1, 2))
    x_copies[2].wait_recv()
    x_copies[3].wait_recv()
    prepare(left)
    @pl.when(c == 1)
    def _():
        for k in range(1, NL):
            value_first(k).wait_recv()

    take_value(0)
    take(2, (3,))
    share(2)
    prepare(right)
    def project_stream(stream, lines, fresh=False):
        def pick(ref, line):
            return ref[line] if stream == 0 else ref[:, line]

        at = [((z, y)[stream] + k) % NL for k in lines]
        rows = jnp.concatenate([pick(NT, line).reshape(LINE, -1) for line in at], axis=0)
        weights = jnp.concatenate(
            [pick(W.at[stream], line).reshape(LINE, -1) for line in at], axis=0
        )
        prod = lax.dot_general(rows, weights, (((0,), (0,)), ((), ())), preferred_element_type=F32)
        qkv[stream] = prod if fresh else qkv[stream] + prod

    def project(lines, fresh=False):
        project_stream(0, lines, fresh)
        project_stream(1, lines, fresh)

    def project_own(lines):
        each_core(lambda core: project_stream(core, lines))

    def project_other(lines):
        each_core(lambda core: project_stream(1 - core, lines))

    take(3, (0, 1))
    fwd0.wait_recv()
    fwd1.wait_recv()
    prepare(across)
    from_other(0)
    from_other(1)
    project((0, 1, 7), True)
    from_other(2)
    project((2, 6))
    take_value(1)
    take(3, (2, 3))
    share(3)
    take(4, range(4))
    rows_copy = remote(TH.at[1 - c], TH_in, ths, thr, sibling, t)
    rows_copy.start()
    project_own((3, 5, 4))
    from_other(3)
    project_other((3, 5))

    take_value(2)
    tab_copy.wait_recv()
    info = []
    for block in range(GEN_BLK):
        flag, segment, place = held(block)
        there = tab_in[block : block + 1, :]
        info.append((
            flag + there,
            there,
            segment + tab_in[GEN_BLK + block : GEN_BLK + block + 1, :],
            place + tab_in[2 * GEN_BLK + block : 2 * GEN_BLK + block + 1, :],
        ))
    q_in = lax.broadcasted_iota(jnp.int32, (BLK, BLK), 0)
    k_in = lax.broadcasted_iota(jnp.int32, (BLK, BLK), 1)
    for i in range(GEN_BLK):
        for j in range(GEN_BLK):
            fi, li, si, pi = info[i]
            fj, lj, sj, pj = info[j]
            both = (fi > 0) & (fj > 0) & (li == lj) & (si == sj)
            meet = jnp.broadcast_to(jnp.where(both, 1, 0), (BLK, BLK))
            ordered = (pi * BLK + q_in) >= (pj * BLK + k_in)
            allow[i * BLK : (i + 1) * BLK, j * BLK : (j + 1) * BLK] = jnp.where(ordered, meet, 0)

    from_other(4)
    project_other((4,))

    loads["cot"].wait()
    keys = qkv[0, :, 2 * HD :].astype(BF16)
    may = allow[...] > 0
    total = jnp.zeros((GEN_BLK * BLK, HD), F32)
    for head in range(HEADS):
        stream, at = (0, head) if head < 2 else (1, head - 2)
        queries = qkv[stream, :, at * HD : (at + 1) * HD].astype(BF16)
        scores = lax.dot_general(
            queries, keys, (((1,), (1,)), ((), ())), preferred_element_type=F32
        ) * HD ** (-0.5)
        masked = jnp.where(may, scores, -1e30)
        row_max = jnp.max(masked, axis=1, keepdims=True)
        raised = jnp.where(may, jnp.exp(masked - row_max), 0.0)
        denom = jnp.sum(raised, axis=1, keepdims=True)
        denom = jnp.where(denom == 0.0, 1.0, denom)
        prob = (raised / denom).astype(BF16)
        probs[head] = prob
        total = total + lax.dot_general(
            prob, cot[:, head * HD : (head + 1) * HD], (((0,), (0,)), ((), ())),
            preferred_element_type=F32,
        )
    vc[...] = total.astype(BF16)

    vc_copy = remote(vc, vc_in, vcs, vcr, sibling, t)
    vc_copy.start()
    R[...] = jnp.dot(
        TH[c].reshape(NL * NL * PART, -1), vc[...], preferred_element_type=F32
    ).reshape(NL, NL * PART, HD)
    rows_copy.wait_recv()
    vc_copy.wait_recv()

    def both_cores(ks):
        lines = [(a + k) % NL for k in ks]
        rows = jnp.concatenate([TH_in[line].reshape(NL * PART, -1) for line in lines], axis=0)
        prod = jnp.dot(rows, vc_in[...], preferred_element_type=F32)
        return [
            R[line] + prod[i * NL * PART : (i + 1) * NL * PART] for i, line in enumerate(lines)
        ]

    def sum_copy(k):
        return remote(H.at[k], P1.at[k], q1s.at[k], q1r.at[k], first((a + k) % NL), t)

    sums = [sum_copy(k) for k in (1, 2, 3, 5, 6, 7)]
    merge = remote(H.at[4], M, ms, mr, first((a + NL - 1) % NL), t)
    H[4] = both_cores((4,))[0].astype(BF16)
    merge.start()
    part3, part6, part2 = both_cores((3, 6, 2))
    for k, value in ((3, part3), (6, part6), (2, part2)):
        H[k] = value.astype(BF16)
        sum_copy(k).start()
    part5, part1, part7, acc = both_cores((5, 1, 7, 0))
    for k, value in ((1, part1), (7, part7)):
        H[k] = value.astype(BF16)
        sum_copy(k).start()
    merge.wait_recv()
    H[5] = (part5 + M[...].astype(F32)).astype(BF16)
    sum_copy(5).start()
    take_value(3)
    for copy in sums:
        copy.wait_recv()
    for k in (1, 2, 3, 5, 6, 7):
        acc = acc + P1[k].astype(F32)
    F[...] = acc.reshape(NL, PART, HD)
    last = []
    for k in (4, 3, 5, 2, 6, 1, 7):
        copy = remote(F.at[(b + k) % NL], P2.at[k], q2s.at[k], q2r.at[k], second((b + k) % NL), t)
        copy.start()
        last.append(copy)

    take_value(4)

    @pl.when(c == 0)
    def _():
        for part in value_shared:
            value_share(*part).wait_recv()

    values = jnp.zeros((GEN_BLK * BLK, HD), F32)
    for i in range(NL):
        values = values + lax.dot_general(
            NT[i].reshape(LINE, -1), V[i].reshape(LINE, HD), (((0,), (0,)), ((), ())),
            preferred_element_type=F32,
        )
    values = values.astype(BF16)
    for head in range(HEADS):
        att[:, head * HD : (head + 1) * HD] = jnp.dot(
            probs[head], values, preferred_element_type=F32
        ).astype(BF16)

    for copy in last:
        copy.wait_recv()
    out = F[b]
    for k in range(1, NL):
        out = out + P2[k]
    grad[...] = out

    for copy in x_copies + sq_copies + sums + last + [sib_copy, tab_copy, fwd0, fwd1, rows_copy, vc_copy, merge]:
        copy.wait_send()
    for i in range(7):
        along(i).wait_send()
    for k in range(NL):
        own_line(k, 0).wait_send()
        own_line(k, 1).wait_send()

    def all_left(core):
        for part in sent:
            ring(core, *part).wait_send()
        for s in range(4):
            for d in range(min(s + 1, 2)):
                to_sibling(core, d, s).wait_send()
        for j in range(4):
            last_to_sibling(core, j).wait_send()
        if core == 1:
            for k in range(1, NL):
                value_first(k).wait_send()
            for part in value_sent:
                value_ring(*part).wait_send()
            for part in value_shared:
                value_share(*part).wait_send()

    each_core(all_left)


def shards(hidden_rows, cotangent, norm_gain, query_weight, key_weight, value_weight, source, segment, position):
    rows = GEN_BLK * BLK
    vmem = pl.BlockSpec(memory_space=pltpu.VMEM)
    dma = pltpu.SemaphoreType.DMA
    return pl.pallas_call(
        kernel,
        out_shape=(
            jax.ShapeDtypeStruct((rows, HEADS * HD), BF16),
            jax.ShapeDtypeStruct((PART, HD), F32),
        ),
        in_specs=[pl.BlockSpec(memory_space=pltpu.HBM)] * 9,
        out_specs=(vmem, vmem),
        scratch_shapes=[
            pltpu.VMEM((rows, HEADS * HD), BF16),
            pltpu.VMEM((NT_X, 1, SLICE), F32),
            pltpu.VMEM((PART, HEADS * HD), BF16),
            pltpu.VMEM((PART, HD), BF16),
            pltpu.VMEM((PART, HD), BF16),
            pltpu.SMEM((CAP_BLK,), jnp.int32),
            pltpu.SMEM((CAP_BLK,), jnp.int32),
            pltpu.SMEM((CAP_BLK,), jnp.int32),
            pltpu.VMEM((2, NL, NL, CHIP, SW), BF16),
            pltpu.VMEM((NL, NL, CHIP, HD), BF16),
            pltpu.VMEM((NT_X, GEN_BLK, BLK, SLICE), BF16),
            pltpu.VMEM((NL, NL, CHIP, rows), BF16),
            pltpu.VMEM((PART, SW + HD), F32),
            pltpu.VMEM((PART, SW + HD), F32),
            pltpu.VMEM((8, 128), jnp.int32),
            pltpu.VMEM((8, 128), jnp.int32),
            pltpu.VMEM((2, rows, SW), F32),
            pltpu.VMEM((HEADS, rows, rows), BF16),
            pltpu.VMEM((rows, rows), jnp.int32),
            pltpu.VMEM((rows, HD), BF16),
            pltpu.VMEM((8, rows), F32),
            pltpu.VMEM((3, 8, rows), F32),
            pltpu.VMEM((rows, HD), F32),
            pltpu.VMEM((2, NL, NT_X, CHIP, rows), BF16),
            pltpu.VMEM((NL, NT_X, CHIP, rows), BF16),
            pltpu.VMEM((NL, CHIP, rows), F32),
            pltpu.VMEM((rows, HD), BF16),
            pltpu.VMEM((NL, NL * PART, HD), F32),
            pltpu.VMEM((NL, NL * PART, HD), BF16),
            pltpu.VMEM((NL * PART, HD), BF16),
            pltpu.VMEM((NL, NL * PART, HD), BF16),
            pltpu.VMEM((NL, PART, HD), F32),
            pltpu.VMEM((NL, PART, HD), F32),
            dma((10,)),
            dma, dma, dma, dma,
            dma((2, 2)), dma((2, 2)), dma((2,)), dma((2,)),
            dma((3,)), dma((3,)),
            dma((7,)), dma((7,)),
            dma((NL,)), dma((NL,)),
            dma((2, NL)),
            dma((2, 4, 4)), dma((2, 4, 4)),
            dma((2, 4)), dma((2, 4)),
            dma((2, 4)), dma((2, 4)), dma((4,)), dma((4,)),
            dma((2, 5)), dma((2, 5)),
            dma, dma, dma, dma, dma, dma,
            dma((NL,)), dma((NL,)), dma((NL,)), dma((NL,)),
        ],
        compiler_params=pltpu.CompilerParams(
            collective_id=0, has_side_effects=True, vmem_limit_bytes=60 * 1024 * 1024
        ),
    )(
        hidden_rows, cotangent, norm_gain.reshape(NT_X, 1, SLICE), query_weight, key_weight, value_weight,
        source, segment, position,
    )


def solution(mesh):
    return jax.shard_map(
        shards,
        mesh=mesh,
        in_specs=(
            P("fsdp", "tp"),
            P("fsdp", "tp"),
            P(),
            P("fsdp", "tp"),
            P("fsdp", "tp"),
            P("fsdp", "tp"),
            P("fsdp"),
            P("fsdp"),
            P("fsdp"),
        ),
        out_specs=(P("fsdp", "tp"), P("fsdp", "tp")),
        check_vma=False,
    )
```

```python
import functools

import jax
import jax.numpy as jnp
from jax import lax
from jax.experimental import pallas as pl
from jax.experimental.pallas import tpu as pltpu
from jax.sharding import PartitionSpec as P

HD = 128
BLK = 128
GEN_BLK = 2
CAP_BLK = 4
NT_X = 4
NL = 8
NF = 128
CHIP = 80
PART = 40
LINE = NL * CHIP
SLICE = 1280
HEADS = 5
SW = 384
MESH = pl.DeviceIdType.MESH
F32 = jnp.float32
BF16 = jnp.bfloat16

epsilon = 1e-06


def kernel(
    hid, cot_in, gain_in, wq_in, wk_in, wv_in, src_in, seg_in, pos_in,
    att, grad,
    cot, gain, wq, wk, wv, src, seg, pos,
    W, V, X, NT, stage, sib, tab_out, tab_in, qkv, probs, allow, vc, sq_out, sq_in, scale,
    TH, TH_in, top_rows, vc_in, R, H, P1, F, P2, own_item,
    ld, sib_s, sib_r, tab_s, tab_r, xs, xr, xfs, xfr,
    sqs, sqr, p1s, p1r, v1s, v1r, os, rs, rr, vs, vr, fs, fr, f4s, f4r, gs, gr,
    ths, thr, vcs, vcr, q1s, q1r, q2s, q2r,
):
    g = lax.axis_index("fsdp")
    t = lax.axis_index("tp")
    c = g % 2
    y = (g // 2) % NL
    z = g // (2 * NL)
    a = y + c * (z - y)
    b = z + c * (y - z)

    def first(i):
        return ((z + c * (i - z)) * NL + (i + c * (y - i))) * 2 + c

    def second(i):
        return ((i + c * (z - i)) * NL + (y + c * (i - y))) * 2 + c

    sibling = g + 1 - 2 * c
    before = (g + NF - 1) % NF
    other = (g + NF - 1 + 2 * c) % NF
    right, left, across = (t + 1) % NT_X, (t + NT_X - 1) % NT_X, (t + 2) % NT_X

    barrier = pltpu.get_barrier_semaphore()

    def greet(f, s):
        pl.semaphore_signal(barrier, inc=1, device_id=(f, s), device_id_type=MESH)

    greet(sibling, t)
    greet(other, t)
    for s in (right, left, across):
        greet(g, s)
    for k in (1, 2, NL - 2, NL - 1):
        greet(first((a + k) % NL), t)
    for k in (1, NL - 1):
        greet(second((b + k) % NL), t)

    def remote(source, target, send, recv, f, s):
        return pltpu.make_async_remote_copy(
            src_ref=source, dst_ref=target, send_sem=send, recv_sem=recv,
            device_id=(f, s), device_id_type=MESH,
        )

    loads = {}
    for i, (name, source, target) in enumerate((
        ("wq", wq_in, wq), ("wk", wk_in, wk), ("wv", wv_in, wv),
        ("src", src_in, src), ("seg", seg_in, seg), ("pos", pos_in, pos),
        ("gain", gain_in, gain),
        ("x0", hid.at[pl.ds(0, BLK)], X.at[t, 0]), ("x1", hid.at[pl.ds(BLK, BLK)], X.at[t, 1]),
        ("cot", cot_in, cot),
    )):
        loads[name] = pltpu.make_async_copy(source, target, ld.at[i])
        loads[name].start()

    for name in ("wq", "wk", "wv"):
        loads[name].wait()
    stream0 = jnp.concatenate([wq[:, : 2 * HD].astype(F32), wk[...].astype(F32)], axis=1)
    stream1 = wq[:, 2 * HD :].astype(F32)
    value_rows = wv[...].astype(F32)
    stage[:, :SW] = jnp.where(c == 0, stream1, stream0)
    stage[:, SW:] = value_rows

    for name in ("src", "seg", "pos"):
        loads[name].wait()

    def held(block):
        flag = jnp.int32(0)
        segment = jnp.int32(0)
        place = jnp.int32(0)
        for s in range(CAP_BLK):
            hit = src[s] == block
            flag = flag + jnp.where(hit, 1, 0)
            segment = segment + jnp.where(hit, seg[s], 0)
            place = place + jnp.where(hit, pos[s], 0)
        return flag, segment, place

    row = lax.broadcasted_iota(jnp.int32, (8, 128), 0)
    table = jnp.zeros((8, 128), jnp.int32)
    for block in range(GEN_BLK):
        for item, value in enumerate(held(GEN_BLK + block)):
            table = jnp.where(row == GEN_BLK * item + block, value, table)
    tab_out[...] = table

    for name in ("x0", "x1"):
        loads[name].wait()
    squares = jnp.zeros((GEN_BLK * BLK, 128), F32)
    for j in range(SLICE // 128):
        wide = X[t, :, :, j * 128 : (j + 1) * 128].reshape(GEN_BLK * BLK, 128).astype(F32)
        squares = squares + wide * wide
    own_squares = jnp.sum(squares.T, axis=0, keepdims=True)
    sq_out[...] = jnp.broadcast_to(own_squares, (8, GEN_BLK * BLK))

    pl.semaphore_wait(barrier, 11)

    sib_copy = remote(stage, sib, sib_s, sib_r, sibling, t)
    sib_copy.start()
    sq_copies = [
        remote(sq_out, sq_in.at[i], sqs.at[i], sqr.at[i], g, s)
        for i, s in enumerate((right, left, across))
    ]
    for copy in sq_copies:
        copy.start()
    x_copies = []
    for d, h in ((0, 0), (1, 1), (0, 1), (1, 0)):
        copy = remote(
            hid.at[pl.ds(BLK * h, BLK)], X.at[t, h], xs.at[d, h], xr.at[d, h], g, (right, left)[d]
        )
        copy.start()
        x_copies.append(copy)
    tab_copy = remote(tab_out, tab_in, tab_s, tab_r, before, t)
    tab_copy.start()

    sib_copy.wait_recv()
    mine = jnp.where(c == 0, stream0, stream1)
    theirs = sib[:, :SW]
    top = jnp.where(c == 0, mine, theirs)
    bottom = jnp.where(c == 0, theirs, mine)
    W[c, z, y] = jnp.concatenate([top, bottom], axis=0).astype(BF16)

    def each_core(body):
        for core in range(2):

            @pl.when(c == core)
            def _(core=core):
                body(core)

    def block_ref(item):
        return W.at[c, z + c * (item - z), item + c * (y - item)]

    def along(i):
        whose, to = ((0, 1), (0, 7), (0, 2), (0, 6), (6, 1), (2, 7), (6, 2))[i]
        ref = block_ref((a + whose) % NL)
        return remote(ref, ref, p1s.at[i], p1r.at[i], first((a + to) % NL), t)

    got = (7, 1, 6, 2, 5, 3, 4)

    def along_arrival(i):
        ref = block_ref((a + got[i]) % NL)
        return remote(ref, ref, p1s.at[i], p1r.at[i], first((a + 1) % NL), t)

    def own_line(k, d):
        item = (a + k) % NL
        ref = block_ref(item)
        return remote(
            ref, ref, os.at[d, k], rr.at[d, 0, (item // 2 + 4 - a // 2) % 4],
            second((b + (1, NL - 1)[d]) % NL), t,
        )

    def take_block(i):
        along_arrival(i).wait_recv()
        for relay in ((), (), (4, 6), (5,), (), (), ())[i]:
            along(relay).start()
        own_line(got[i], 0).start()
        own_line(got[i], 1).start()

    for i in range(4):
        along(i).start()
    own_line(0, 0).start()
    own_line(0, 1).start()
    for i in range(4):
        take_block(i)

    def piece(core, line, j):
        items = pl.ds(2 * ((a // 2 + j) % 4), 2)
        return W.at[0, line, items] if core == 0 else W.at[1, items, line]

    def whole(core, line):
        return W.at[0, line] if core == 0 else W.at[1, :, line]

    def ring(core, d, s, j):
        ref = piece(core, (b + (NL - s, s)[d]) % NL, j)
        target = second((b + (1, NL - 1)[d]) % NL)
        return remote(ref, ref, rs.at[d, s, j], rr.at[d, s, j], target, t)

    def arrival(core, d, s, j):
        ref = piece(core, (b + (NL - s, s)[d]) % NL, j)
        target = second((b + (1, NL - 1)[d]) % NL)
        return remote(ref, ref, rs.at[d, s - 1, j], rr.at[d, s - 1, j], target, t)

    def to_sibling(core, d, s):
        ref = whole(core, (b + (NL - s, s)[d]) % NL)
        return remote(ref, ref, fs.at[d, s], fr.at[d, s], sibling, t)

    def from_sibling(core, d, s):
        ref = whole(1 - core, (a + (NL - s, s)[d]) % NL)
        return remote(ref, ref, fs.at[d, s], fr.at[d, s], sibling, t)

    def last_to_sibling(core, j):
        ref = piece(core, (b + 4) % NL, j)
        return remote(ref, ref, f4s.at[j], f4r.at[j], sibling, t)

    def last_from_sibling(core, j):
        items = pl.ds(2 * ((b // 2 + j) % 4), 2)
        line = (a + 4) % NL
        ref = W.at[0, line, items] if core == 1 else W.at[1, items, line]
        return remote(ref, ref, f4s.at[j], f4r.at[j], sibling, t)

    orders = ((0, 1, 3, 2), (0, 3, 2, 1))
    steps = [(d, s, orders[d][i]) for s in range(1, 4) for i in range(4) for d in range(2)]
    last_steps = [(0, 4, 0), (1, 4, 3), (0, 4, 1), (1, 4, 2)]
    sent = [p for p in steps if p[1] < 3 or p[2] in ((0, 1), (3, 2))[p[0]]]

    def take(s, places):
        def body(core):
            for part in steps + last_steps:
                if part[1] == s and orders[part[0]].index(part[2]) in places:
                    arrival(core, *part).wait_recv()
                    if part in sent:
                        ring(core, *part).start()
                    if s == 4:
                        last_to_sibling(core, part[2]).start()

        each_core(body)

    def share(s):
        each_core(lambda core: [to_sibling(core, d, s).start() for d in range(min(s + 1, 2))])

    def from_other(s):
        def body(core):
            if s == 4:
                for j in range(4):
                    last_from_sibling(core, j).wait_recv()
            else:
                for d in range(min(s + 1, 2)):
                    from_sibling(core, d, s).wait_recv()

        each_core(body)

    take(1, (0,))
    for i in range(4, 7):
        take_block(i)
    share(0)

    top = jnp.where(c == 0, value_rows, sib[:, SW:])
    bottom = jnp.where(c == 0, sib[:, SW:], value_rows)

    def value_first(k):
        return remote(
            V.at[z, y], V.at[z, y], v1s.at[k], v1r.at[k], first((a + k) % NL), t
        )

    @pl.when(c == 1)
    def _():
        V[z, y] = jnp.concatenate([top, bottom], axis=0).astype(BF16)
        for k in (1, 7, 2, 6, 3, 5, 4):
            value_first(k).start()

    take(1, (1,))

    x_copies[0].wait_recv()
    fwd0 = remote(X.at[left, 0], X.at[left, 0], xfs.at[0], xfr.at[0], g, right)
    fwd0.start()
    x_copies[1].wait_recv()
    fwd1 = remote(X.at[right, 1], X.at[right, 1], xfs.at[1], xfr.at[1], g, left)
    fwd1.start()

    total = own_squares
    for i, copy in enumerate(sq_copies):
        copy.wait_recv()
        total = total + sq_in[i, :1, :]
    by_token = lax.rsqrt(total / (NT_X * SLICE) + epsilon)
    scale[...] = jnp.broadcast_to(by_token, (128, GEN_BLK * BLK)).T

    def prepare(s):
        for i in range(2):
            blocks = []
            for j in range(5):
                columns = pl.ds(i * LINE + j * 128, 128)
                wide = X[s, :, :, columns].reshape(GEN_BLK * BLK, 128).astype(F32)
                blocks.append((wide * scale[...] * gain[s, :, columns]).T)
            line = jnp.concatenate(blocks, axis=0).reshape(NL, CHIP, GEN_BLK * BLK)
            NT[2 * s + i] = line.astype(BF16)
            TH[1, 2 * s + i] = line[:, PART:].reshape(NT_X, CHIP, -1).astype(BF16)
            top_rows[:, i * PART : (i + 1) * PART, :] = line[:, :PART]
        TH[0, :, s] = top_rows[...].astype(BF16)

    loads["gain"].wait()
    prepare(t)
    take(1, (2, 3))
    share(1)
    def value_line(at, d, s):
        return V.at[:, (at + (NL - s, s)[d]) % NL]

    def value_ring(d, s):
        ref = value_line(b, d, s)
        return remote(ref, ref, vs.at[d, s], vr.at[d, s], second((b + (1, NL - 1)[d]) % NL), t)

    def value_arrival(d, s):
        ref = value_line(b, d, s)
        return remote(
            ref, ref, vs.at[d, s - 1], vr.at[d, s - 1], second((b + (1, NL - 1)[d]) % NL), t
        )

    def value_share(d, s):
        ref = value_line(y, d, s)
        return remote(ref, ref, gs.at[d, s], gr.at[d, s], sibling, t)

    value_steps = [(0, 0), (1, 0), (0, 1), (1, 1), (0, 2), (1, 2), (0, 3), (1, 3), (0, 4)]
    value_sent = [p for p in value_steps if p[1] < (4, 3)[p[0]]]
    value_shared = [p for p in value_steps if p != (1, 0)]

    def take_value(s):
        @pl.when(c == 1)
        def _():
            for part in value_steps:
                if part[1] == s:
                    if s > 0:
                        value_arrival(*part).wait_recv()
                    if part in value_sent:
                        value_ring(*part).start()
                    if part in value_shared:
                        value_share(*part).start()

    take(2, (0, 1, 2))
    x_copies[2].wait_recv()
    x_copies[3].wait_recv()
    prepare(left)
    @pl.when(c == 1)
    def _():
        for k in range(1, NL):
            value_first(k).wait_recv()

    take_value(0)
    take(2, (3,))
    share(2)
    prepare(right)
    def project_stream(stream, lines, fresh=False):
        def pick(ref, line):
            return ref[line] if stream == 0 else ref[:, line]

        at = [((z, y)[stream] + k) % NL for k in lines]
        rows = jnp.concatenate([pick(NT, line).reshape(LINE, -1) for line in at], axis=0)
        weights = jnp.concatenate(
            [pick(W.at[stream], line).reshape(LINE, -1) for line in at], axis=0
        )
        prod = lax.dot_general(rows, weights, (((0,), (0,)), ((), ())), preferred_element_type=F32)
        qkv[stream] = prod if fresh else qkv[stream] + prod

    def project(lines, fresh=False):
        project_stream(0, lines, fresh)
        project_stream(1, lines, fresh)

    def project_own(lines):
        each_core(lambda core: project_stream(core, lines))

    def project_other(lines):
        each_core(lambda core: project_stream(1 - core, lines))

    take(3, (0, 1))
    fwd0.wait_recv()
    fwd1.wait_recv()
    prepare(across)
    from_other(0)
    from_other(1)
    project((0, 1, 7), True)
    from_other(2)
    project((2, 6))
    take_value(1)
    take(3, (2, 3))
    share(3)
    take(4, range(4))
    rows_copy = remote(TH.at[1 - c], TH_in, ths, thr, sibling, t)
    rows_copy.start()
    project_own((3, 5, 4))
    from_other(3)
    project_other((3, 5))

    take_value(2)
    tab_copy.wait_recv()
    info = []
    for block in range(GEN_BLK):
        flag, segment, place = held(block)
        there = tab_in[block : block + 1, :]
        info.append((
            flag + there,
            there,
            segment + tab_in[GEN_BLK + block : GEN_BLK + block + 1, :],
            place + tab_in[2 * GEN_BLK + block : 2 * GEN_BLK + block + 1, :],
        ))
    q_in = lax.broadcasted_iota(jnp.int32, (BLK, BLK), 0)
    k_in = lax.broadcasted_iota(jnp.int32, (BLK, BLK), 1)
    for i in range(GEN_BLK):
        for j in range(GEN_BLK):
            fi, li, si, pi = info[i]
            fj, lj, sj, pj = info[j]
            both = (fi > 0) & (fj > 0) & (li == lj) & (si == sj)
            meet = jnp.broadcast_to(jnp.where(both, 1, 0), (BLK, BLK))
            ordered = (pi * BLK + q_in) >= (pj * BLK + k_in)
            allow[i * BLK : (i + 1) * BLK, j * BLK : (j + 1) * BLK] = jnp.where(ordered, meet, 0)

    from_other(4)
    project_other((4,))

    loads["cot"].wait()
    keys = qkv[0, :, 2 * HD :].astype(BF16)
    may = allow[...] > 0
    total = jnp.zeros((GEN_BLK * BLK, HD), F32)
    for head in range(HEADS):
        stream, at = (0, head) if head < 2 else (1, head - 2)
        queries = qkv[stream, :, at * HD : (at + 1) * HD].astype(BF16)
        scores = lax.dot_general(
            queries, keys, (((1,), (1,)), ((), ())), preferred_element_type=F32
        ) * HD ** (-0.5)
        masked = jnp.where(may, scores, -1e30)
        row_max = jnp.max(masked, axis=1, keepdims=True)
        raised = jnp.where(may, jnp.exp(masked - row_max), 0.0)
        denom = jnp.sum(raised, axis=1, keepdims=True)
        denom = jnp.where(denom == 0.0, 1.0, denom)
        prob = (raised / denom).astype(BF16)
        probs[head] = prob
        total = total + lax.dot_general(
            prob, cot[:, head * HD : (head + 1) * HD], (((0,), (0,)), ((), ())),
            preferred_element_type=F32,
        )
    vc[...] = total.astype(BF16)

    vc_copy = remote(vc, vc_in, vcs, vcr, sibling, t)
    vc_copy.start()
    R[...] = jnp.dot(
        TH[c].reshape(NL * NL * PART, -1), vc[...], preferred_element_type=F32
    ).reshape(NL, NL * PART, HD)
    rows_copy.wait_recv()
    vc_copy.wait_recv()

    def both_cores(ks):
        lines = [(a + k) % NL for k in ks]
        rows = jnp.concatenate([TH_in[line].reshape(NL * PART, -1) for line in lines], axis=0)
        prod = jnp.dot(rows, vc_in[...], preferred_element_type=F32)
        return [
            R[line] + prod[i * NL * PART : (i + 1) * NL * PART] for i, line in enumerate(lines)
        ]

    def sum_copy(k):
        return remote(H.at[k], P1.at[k], q1s.at[k], q1r.at[k], first((a + k) % NL), t)

    sums = [sum_copy(k) for k in range(1, NL)]
    for ks in ((4,), (3, 5), (2, 6)):
        for k, value in zip(ks, both_cores(ks)):
            H[k] = value.astype(BF16)
            sum_copy(k).start()
    part1, part7, acc = both_cores((1, 7, 0))
    for k, value in ((1, part1), (7, part7)):
        H[k] = value.astype(BF16)
        sum_copy(k).start()
    take_value(3)
    for copy in sums:
        copy.wait_recv()
    for k in range(1, NL):
        acc = acc + P1[k].astype(F32)
    items = acc.reshape(NL, PART, HD)
    F[...] = jnp.concatenate([items, items[:, :8]], axis=1).astype(BF16)
    own_item[...] = jnp.sum(
        jnp.where(lax.broadcasted_iota(jnp.int32, (NL, 1, 1), 0) == b, items, 0.0), axis=0
    )
    last = []
    for k in (4, 3, 5, 2, 6, 1, 7):
        copy = remote(F.at[(b + k) % NL], P2.at[k], q2s.at[k], q2r.at[k], second((b + k) % NL), t)
        copy.start()
        last.append(copy)

    take_value(4)

    @pl.when(c == 0)
    def _():
        for part in value_shared:
            value_share(*part).wait_recv()

    values = jnp.zeros((GEN_BLK * BLK, HD), F32)
    for i in range(NL):
        values = values + lax.dot_general(
            NT[i].reshape(LINE, -1), V[i].reshape(LINE, HD), (((0,), (0,)), ((), ())),
            preferred_element_type=F32,
        )
    values = values.astype(BF16)
    for head in range(HEADS):
        att[:, head * HD : (head + 1) * HD] = jnp.dot(
            probs[head], values, preferred_element_type=F32
        ).astype(BF16)

    for copy in x_copies + sq_copies + sums + [sib_copy, tab_copy, fwd0, fwd1, rows_copy, vc_copy]:
        copy.wait_send()
    for i in range(7):
        along(i).wait_send()
    for k in range(NL):
        own_line(k, 0).wait_send()
        own_line(k, 1).wait_send()

    def all_left(core):
        for part in sent:
            ring(core, *part).wait_send()
        for s in range(4):
            for d in range(min(s + 1, 2)):
                to_sibling(core, d, s).wait_send()
        for j in range(4):
            last_to_sibling(core, j).wait_send()
        if core == 1:
            for k in range(1, NL):
                value_first(k).wait_send()
            for part in value_sent:
                value_ring(*part).wait_send()
            for part in value_shared:
                value_share(*part).wait_send()

    each_core(all_left)

    for copy in last:
        copy.wait_recv()
    out = own_item[...]
    for k in range(1, NL):
        out = out + P2[k].astype(F32)[:PART]
    grad[...] = out

    for copy in last:
        copy.wait_send()


def hand_over(att, grad, att_out, grad_out, att_held, grad_held, read, write):
    whole = pl.ds(0, PART)
    pieces = [(grad, grad_held, grad_out, whole)]
    for i in range(4):
        pieces.append((att, att_held, att_out, pl.ds(64 * i, 64)))
    reads = [
        pltpu.make_async_copy(source.at[rows], held.at[rows], read.at[i])
        for i, (source, held, _, rows) in enumerate(pieces)
    ]
    writes = [
        pltpu.make_async_copy(held.at[rows], target.at[rows], write.at[i])
        for i, (_, held, target, rows) in enumerate(pieces)
    ]
    for copy in reads:
        copy.start()
    for one, two in zip(reads, writes):
        one.wait()
        two.start()
    for copy in writes:
        copy.wait()


def shards(hidden_rows, cotangent, norm_gain, query_weight, key_weight, value_weight, source, segment, position):
    rows = GEN_BLK * BLK
    vmem = pl.BlockSpec(memory_space=pltpu.VMEM)
    dma = pltpu.SemaphoreType.DMA
    made = pl.pallas_call(
        kernel,
        out_shape=(
            jax.ShapeDtypeStruct((rows, HEADS * HD), BF16),
            jax.ShapeDtypeStruct((PART, HD), F32),
        ),
        in_specs=[pl.BlockSpec(memory_space=pltpu.HBM)] * 9,
        out_specs=(vmem, vmem),
        scratch_shapes=[
            pltpu.VMEM((rows, HEADS * HD), BF16),
            pltpu.VMEM((NT_X, 1, SLICE), F32),
            pltpu.VMEM((PART, HEADS * HD), BF16),
            pltpu.VMEM((PART, HD), BF16),
            pltpu.VMEM((PART, HD), BF16),
            pltpu.SMEM((CAP_BLK,), jnp.int32),
            pltpu.SMEM((CAP_BLK,), jnp.int32),
            pltpu.SMEM((CAP_BLK,), jnp.int32),
            pltpu.VMEM((2, NL, NL, CHIP, SW), BF16),
            pltpu.VMEM((NL, NL, CHIP, HD), BF16),
            pltpu.VMEM((NT_X, GEN_BLK, BLK, SLICE), BF16),
            pltpu.VMEM((NL, NL, CHIP, rows), BF16),
            pltpu.VMEM((PART, SW + HD), F32),
            pltpu.VMEM((PART, SW + HD), F32),
            pltpu.VMEM((8, 128), jnp.int32),
            pltpu.VMEM((8, 128), jnp.int32),
            pltpu.VMEM((2, rows, SW), F32),
            pltpu.VMEM((HEADS, rows, rows), BF16),
            pltpu.VMEM((rows, rows), jnp.int32),
            pltpu.VMEM((rows, HD), BF16),
            pltpu.VMEM((8, rows), F32),
            pltpu.VMEM((3, 8, rows), F32),
            pltpu.VMEM((rows, HD), F32),
            pltpu.VMEM((2, NL, NT_X, CHIP, rows), BF16),
            pltpu.VMEM((NL, NT_X, CHIP, rows), BF16),
            pltpu.VMEM((NL, CHIP, rows), F32),
            pltpu.VMEM((rows, HD), BF16),
            pltpu.VMEM((NL, NL * PART, HD), F32),
            pltpu.VMEM((NL, NL * PART, HD), BF16),
            pltpu.VMEM((NL, NL * PART, HD), BF16),
            pltpu.VMEM((NL, PART + 8, HD), BF16),
            pltpu.VMEM((NL, PART + 8, HD), BF16),
            pltpu.VMEM((PART, HD), F32),
            dma((10,)),
            dma, dma, dma, dma,
            dma((2, 2)), dma((2, 2)), dma((2,)), dma((2,)),
            dma((3,)), dma((3,)),
            dma((7,)), dma((7,)),
            dma((NL,)), dma((NL,)),
            dma((2, NL)),
            dma((2, 4, 4)), dma((2, 4, 4)),
            dma((2, 4)), dma((2, 4)),
            dma((2, 4)), dma((2, 4)), dma((4,)), dma((4,)),
            dma((2, 5)), dma((2, 5)),
            dma, dma, dma, dma,
            dma((NL,)), dma((NL,)), dma((NL,)), dma((NL,)),
        ],
        compiler_params=pltpu.CompilerParams(
            collective_id=0, has_side_effects=True, vmem_limit_bytes=60 * 1024 * 1024
        ),
    )(
        hidden_rows, cotangent, norm_gain.reshape(NT_X, 1, SLICE), query_weight, key_weight, value_weight,
        source, segment, position,
    )
    hbm = pl.BlockSpec(memory_space=pltpu.HBM)
    return pl.pallas_call(
        hand_over,
        out_shape=tuple(jax.ShapeDtypeStruct(one.shape, one.dtype) for one in made),
        in_specs=[hbm, hbm],
        out_specs=(hbm, hbm),
        scratch_shapes=[
            pltpu.VMEM(made[0].shape, BF16),
            pltpu.VMEM(made[1].shape, F32),
            dma((5,)),
            dma((5,)),
        ],
        compiler_params=pltpu.CompilerParams(vmem_limit_bytes=60 * 1024 * 1024),
    )(*made)


def solution(mesh):
    return jax.shard_map(
        shards,
        mesh=mesh,
        in_specs=(
            P("fsdp", "tp"),
            P("fsdp", "tp"),
            P(),
            P("fsdp", "tp"),
            P("fsdp", "tp"),
            P("fsdp", "tp"),
            P("fsdp"),
            P("fsdp"),
            P("fsdp"),
        ),
        out_specs=(P("fsdp", "tp"), P("fsdp", "tp")),
        check_vma=False,
    )
```

```python
import functools

import jax
import jax.numpy as jnp
from jax import lax
from jax.experimental import pallas as pl
from jax.experimental.pallas import tpu as pltpu
from jax.sharding import PartitionSpec as P

HD = 128
BLK = 128
GEN_BLK = 2
CAP_BLK = 4
NT_X = 4
NL = 8
NF = 128
CHIP = 80
PART = 40
LINE = NL * CHIP
SLICE = 1280
HEADS = 5
SW = 384
MESH = pl.DeviceIdType.MESH
F32 = jnp.float32
BF16 = jnp.bfloat16

epsilon = 1e-06


def kernel(
    hid, cot_in, gain_in, wq_in, wk_in, wv_in, src_in, seg_in, pos_in,
    att, grad,
    cot, gain, wq, wk, wv, src, seg, pos,
    W, V, X, NT, stage, sib, tab_out, tab_in, qkv, probs, allow, vc, sq_out, sq_in, scale,
    TH, TH_in, top_rows, vc_in, R, H, P1, F, P2, own_item,
    ld, sib_s, sib_r, tab_s, tab_r, xs, xr, xfs, xfr,
    sqs, sqr, p1s, p1r, v1s, v1r, os, rs, rr, vs, vr, fs, fr, f4s, f4r, gs, gr,
    ths, thr, vcs, vcr, q1s, q1r, q2s, q2r,
):
    g = lax.axis_index("fsdp")
    t = lax.axis_index("tp")
    c = g % 2
    y = (g // 2) % NL
    z = g // (2 * NL)
    a = y + c * (z - y)
    b = z + c * (y - z)

    def first(i):
        return ((z + c * (i - z)) * NL + (i + c * (y - i))) * 2 + c

    def second(i):
        return ((i + c * (z - i)) * NL + (y + c * (i - y))) * 2 + c

    sibling = g + 1 - 2 * c
    before = (g + NF - 1) % NF
    other = (g + NF - 1 + 2 * c) % NF
    right, left, across = (t + 1) % NT_X, (t + NT_X - 1) % NT_X, (t + 2) % NT_X

    barrier = pltpu.get_barrier_semaphore()

    def greet(f, s):
        pl.semaphore_signal(barrier, inc=1, device_id=(f, s), device_id_type=MESH)

    greet(sibling, t)
    greet(other, t)
    for s in (right, left, across):
        greet(g, s)
    for k in (1, 2, NL - 2, NL - 1):
        greet(first((a + k) % NL), t)
    for k in (1, NL - 1):
        greet(second((b + k) % NL), t)

    def remote(source, target, send, recv, f, s):
        return pltpu.make_async_remote_copy(
            src_ref=source, dst_ref=target, send_sem=send, recv_sem=recv,
            device_id=(f, s), device_id_type=MESH,
        )

    loads = {}
    for i, (name, source, target) in enumerate((
        ("wq", wq_in, wq), ("wk", wk_in, wk), ("wv", wv_in, wv),
        ("src", src_in, src), ("seg", seg_in, seg), ("pos", pos_in, pos),
        ("gain", gain_in, gain),
        ("x0", hid.at[pl.ds(0, BLK)], X.at[t, 0]), ("x1", hid.at[pl.ds(BLK, BLK)], X.at[t, 1]),
        ("cot", cot_in, cot),
    )):
        loads[name] = pltpu.make_async_copy(source, target, ld.at[i])
        loads[name].start()

    for name in ("wq", "wk", "wv"):
        loads[name].wait()
    stream0 = jnp.concatenate([wq[:, : 2 * HD].astype(F32), wk[...].astype(F32)], axis=1)
    stream1 = wq[:, 2 * HD :].astype(F32)
    value_rows = wv[...].astype(F32)
    stage[:, :SW] = jnp.where(c == 0, stream1, stream0)
    stage[:, SW:] = value_rows

    for name in ("src", "seg", "pos"):
        loads[name].wait()

    def held(block):
        flag = jnp.int32(0)
        segment = jnp.int32(0)
        place = jnp.int32(0)
        for s in range(CAP_BLK):
            hit = src[s] == block
            flag = flag + jnp.where(hit, 1, 0)
            segment = segment + jnp.where(hit, seg[s], 0)
            place = place + jnp.where(hit, pos[s], 0)
        return flag, segment, place

    row = lax.broadcasted_iota(jnp.int32, (8, 128), 0)
    table = jnp.zeros((8, 128), jnp.int32)
    for block in range(GEN_BLK):
        for item, value in enumerate(held(GEN_BLK + block)):
            table = jnp.where(row == GEN_BLK * item + block, value, table)
    tab_out[...] = table

    for name in ("x0", "x1"):
        loads[name].wait()
    squares = jnp.zeros((GEN_BLK * BLK, 128), F32)
    for j in range(SLICE // 128):
        wide = X[t, :, :, j * 128 : (j + 1) * 128].reshape(GEN_BLK * BLK, 128).astype(F32)
        squares = squares + wide * wide
    own_squares = jnp.sum(squares.T, axis=0, keepdims=True)
    sq_out[...] = jnp.broadcast_to(own_squares, (8, GEN_BLK * BLK))

    pl.semaphore_wait(barrier, 11)

    sib_copy = remote(stage, sib, sib_s, sib_r, sibling, t)
    sib_copy.start()
    sq_copies = [
        remote(sq_out, sq_in.at[i], sqs.at[i], sqr.at[i], g, s)
        for i, s in enumerate((right, left, across))
    ]
    for copy in sq_copies:
        copy.start()
    x_copies = []
    for d, h in ((0, 0), (1, 1), (0, 1), (1, 0)):
        copy = remote(
            hid.at[pl.ds(BLK * h, BLK)], X.at[t, h], xs.at[d, h], xr.at[d, h], g, (right, left)[d]
        )
        copy.start()
        x_copies.append(copy)
    tab_copy = remote(tab_out, tab_in, tab_s, tab_r, before, t)
    tab_copy.start()

    sib_copy.wait_recv()
    mine = jnp.where(c == 0, stream0, stream1)
    theirs = sib[:, :SW]
    top = jnp.where(c == 0, mine, theirs)
    bottom = jnp.where(c == 0, theirs, mine)
    W[c, z, y] = jnp.concatenate([top, bottom], axis=0).astype(BF16)

    def each_core(body):
        for core in range(2):

            @pl.when(c == core)
            def _(core=core):
                body(core)

    def block_ref(item):
        return W.at[c, z + c * (item - z), item + c * (y - item)]

    def along(i):
        whose, to = ((0, 1), (0, 7), (0, 2), (0, 6), (6, 1), (2, 7), (6, 2))[i]
        ref = block_ref((a + whose) % NL)
        return remote(ref, ref, p1s.at[i], p1r.at[i], first((a + to) % NL), t)

    got = (7, 1, 6, 2, 5, 3, 4)

    def along_arrival(i):
        ref = block_ref((a + got[i]) % NL)
        return remote(ref, ref, p1s.at[i], p1r.at[i], first((a + 1) % NL), t)

    def own_line(k, d):
        item = (a + k) % NL
        ref = block_ref(item)
        return remote(
            ref, ref, os.at[d, k], rr.at[d, 0, (item // 2 + 4 - a // 2) % 4],
            second((b + (1, NL - 1)[d]) % NL), t,
        )

    def take_block(i):
        along_arrival(i).wait_recv()
        for relay in ((), (), (4, 6), (5,), (), (), ())[i]:
            along(relay).start()
        own_line(got[i], 0).start()
        own_line(got[i], 1).start()

    for i in range(4):
        along(i).start()
    own_line(0, 0).start()
    own_line(0, 1).start()
    for i in range(4):
        take_block(i)

    def piece(core, line, j):
        items = pl.ds(2 * ((a // 2 + j) % 4), 2)
        return W.at[0, line, items] if core == 0 else W.at[1, items, line]

    def whole(core, line):
        return W.at[0, line] if core == 0 else W.at[1, :, line]

    def ring(core, d, s, j):
        ref = piece(core, (b + (NL - s, s)[d]) % NL, j)
        target = second((b + (1, NL - 1)[d]) % NL)
        return remote(ref, ref, rs.at[d, s, j], rr.at[d, s, j], target, t)

    def arrival(core, d, s, j):
        ref = piece(core, (b + (NL - s, s)[d]) % NL, j)
        target = second((b + (1, NL - 1)[d]) % NL)
        return remote(ref, ref, rs.at[d, s - 1, j], rr.at[d, s - 1, j], target, t)

    def to_sibling(core, d, s):
        ref = whole(core, (b + (NL - s, s)[d]) % NL)
        return remote(ref, ref, fs.at[d, s], fr.at[d, s], sibling, t)

    def from_sibling(core, d, s):
        ref = whole(1 - core, (a + (NL - s, s)[d]) % NL)
        return remote(ref, ref, fs.at[d, s], fr.at[d, s], sibling, t)

    def last_to_sibling(core, j):
        ref = piece(core, (b + 4) % NL, j)
        return remote(ref, ref, f4s.at[j], f4r.at[j], sibling, t)

    def last_from_sibling(core, j):
        items = pl.ds(2 * ((b // 2 + j) % 4), 2)
        line = (a + 4) % NL
        ref = W.at[0, line, items] if core == 1 else W.at[1, items, line]
        return remote(ref, ref, f4s.at[j], f4r.at[j], sibling, t)

    orders = ((0, 1, 3, 2), (0, 3, 2, 1))
    steps = [(d, s, orders[d][i]) for s in range(1, 4) for i in range(4) for d in range(2)]
    last_steps = [(0, 4, 0), (1, 4, 3), (0, 4, 1), (1, 4, 2)]
    sent = [p for p in steps if p[1] < 3 or p[2] in ((0, 1), (3, 2))[p[0]]]

    def take(s, places):
        def body(core):
            for part in steps + last_steps:
                if part[1] == s and orders[part[0]].index(part[2]) in places:
                    arrival(core, *part).wait_recv()
                    if part in sent:
                        ring(core, *part).start()
                    if s == 4:
                        last_to_sibling(core, part[2]).start()

        each_core(body)

    def share(s):
        each_core(lambda core: [to_sibling(core, d, s).start() for d in range(min(s + 1, 2))])

    def from_other(s):
        def body(core):
            if s == 4:
                for j in range(4):
                    last_from_sibling(core, j).wait_recv()
            else:
                for d in range(min(s + 1, 2)):
                    from_sibling(core, d, s).wait_recv()

        each_core(body)

    take(1, (0,))
    for i in range(4, 7):
        take_block(i)
    share(0)

    top = jnp.where(c == 0, value_rows, sib[:, SW:])
    bottom = jnp.where(c == 0, sib[:, SW:], value_rows)

    def value_first(k):
        return remote(
            V.at[z, y], V.at[z, y], v1s.at[k], v1r.at[k], first((a + k) % NL), t
        )

    @pl.when(c == 1)
    def _():
        V[z, y] = jnp.concatenate([top, bottom], axis=0).astype(BF16)
        for k in (1, 7, 2, 6, 3, 5, 4):
            value_first(k).start()

    take(1, (1,))

    x_copies[0].wait_recv()
    fwd0 = remote(X.at[left, 0], X.at[left, 0], xfs.at[0], xfr.at[0], g, right)
    fwd0.start()
    x_copies[1].wait_recv()
    fwd1 = remote(X.at[right, 1], X.at[right, 1], xfs.at[1], xfr.at[1], g, left)
    fwd1.start()

    total = own_squares
    for i, copy in enumerate(sq_copies):
        copy.wait_recv()
        total = total + sq_in[i, :1, :]
    by_token = lax.rsqrt(total / (NT_X * SLICE) + epsilon)
    scale[...] = jnp.broadcast_to(by_token, (128, GEN_BLK * BLK)).T

    def prepare(s):
        for i in range(2):
            blocks = []
            for j in range(5):
                columns = pl.ds(i * LINE + j * 128, 128)
                wide = X[s, :, :, columns].reshape(GEN_BLK * BLK, 128).astype(F32)
                blocks.append((wide * scale[...] * gain[s, :, columns]).T)
            line = jnp.concatenate(blocks, axis=0).reshape(NL, CHIP, GEN_BLK * BLK)
            NT[2 * s + i] = line.astype(BF16)
            TH[1, 2 * s + i] = line[:, PART:].reshape(NT_X, CHIP, -1).astype(BF16)
            top_rows[:, i * PART : (i + 1) * PART, :] = line[:, :PART]
        TH[0, :, s] = top_rows[...].astype(BF16)

    loads["gain"].wait()
    prepare(t)
    take(1, (2, 3))
    share(1)
    def value_line(at, d, s):
        return V.at[:, (at + (NL - s, s)[d]) % NL]

    def value_ring(d, s):
        ref = value_line(b, d, s)
        return remote(ref, ref, vs.at[d, s], vr.at[d, s], second((b + (1, NL - 1)[d]) % NL), t)

    def value_arrival(d, s):
        ref = value_line(b, d, s)
        return remote(
            ref, ref, vs.at[d, s - 1], vr.at[d, s - 1], second((b + (1, NL - 1)[d]) % NL), t
        )

    def value_share(d, s):
        ref = value_line(y, d, s)
        return remote(ref, ref, gs.at[d, s], gr.at[d, s], sibling, t)

    value_steps = [(0, 0), (1, 0), (0, 1), (1, 1), (0, 2), (1, 2), (0, 3), (1, 3), (0, 4)]
    value_sent = [p for p in value_steps if p[1] < (4, 3)[p[0]]]
    value_shared = [p for p in value_steps if p != (1, 0)]

    def take_value(s):
        @pl.when(c == 1)
        def _():
            for part in value_steps:
                if part[1] == s:
                    if s > 0:
                        value_arrival(*part).wait_recv()
                    if part in value_sent:
                        value_ring(*part).start()
                    if part in value_shared:
                        value_share(*part).start()

    take(2, (0, 1, 2))
    x_copies[2].wait_recv()
    x_copies[3].wait_recv()
    prepare(left)
    @pl.when(c == 1)
    def _():
        for k in range(1, NL):
            value_first(k).wait_recv()

    take_value(0)
    take(2, (3,))
    share(2)
    prepare(right)
    def project_stream(stream, lines, fresh=False):
        def pick(ref, line):
            return ref[line] if stream == 0 else ref[:, line]

        at = [((z, y)[stream] + k) % NL for k in lines]
        rows = jnp.concatenate([pick(NT, line).reshape(LINE, -1) for line in at], axis=0)
        weights = jnp.concatenate(
            [pick(W.at[stream], line).reshape(LINE, -1) for line in at], axis=0
        )
        prod = lax.dot_general(rows, weights, (((0,), (0,)), ((), ())), preferred_element_type=F32)
        qkv[stream] = prod if fresh else qkv[stream] + prod

    def project(lines, fresh=False):
        project_stream(0, lines, fresh)
        project_stream(1, lines, fresh)

    def project_own(lines):
        each_core(lambda core: project_stream(core, lines))

    def project_other(lines):
        each_core(lambda core: project_stream(1 - core, lines))

    take(3, (0, 1))
    fwd0.wait_recv()
    fwd1.wait_recv()
    prepare(across)
    from_other(0)
    from_other(1)
    project((0, 1, 7), True)
    from_other(2)
    project((2, 6))
    take_value(1)
    take(3, (2, 3))
    share(3)
    take(4, range(4))
    rows_copy = remote(TH.at[1 - c], TH_in, ths, thr, sibling, t)
    rows_copy.start()
    project_own((3, 5, 4))
    from_other(3)
    project_other((3, 5))

    tab_copy.wait_recv()
    info = []
    for block in range(GEN_BLK):
        flag, segment, place = held(block)
        there = tab_in[block : block + 1, :]
        info.append((
            flag + there,
            there,
            segment + tab_in[GEN_BLK + block : GEN_BLK + block + 1, :],
            place + tab_in[2 * GEN_BLK + block : 2 * GEN_BLK + block + 1, :],
        ))
    q_in = lax.broadcasted_iota(jnp.int32, (BLK, BLK), 0)
    k_in = lax.broadcasted_iota(jnp.int32, (BLK, BLK), 1)
    for i in range(GEN_BLK):
        for j in range(GEN_BLK):
            fi, li, si, pi = info[i]
            fj, lj, sj, pj = info[j]
            both = (fi > 0) & (fj > 0) & (li == lj) & (si == sj)
            meet = jnp.broadcast_to(jnp.where(both, 1, 0), (BLK, BLK))
            ordered = (pi * BLK + q_in) >= (pj * BLK + k_in)
            allow[i * BLK : (i + 1) * BLK, j * BLK : (j + 1) * BLK] = jnp.where(ordered, meet, 0)

    from_other(4)
    project_other((4,))

    loads["cot"].wait()
    keys = qkv[0, :, 2 * HD :].astype(BF16)
    may = allow[...] > 0
    total = jnp.zeros((GEN_BLK * BLK, HD), F32)
    for head in range(HEADS):
        stream, at = (0, head) if head < 2 else (1, head - 2)
        queries = qkv[stream, :, at * HD : (at + 1) * HD].astype(BF16)
        scores = lax.dot_general(
            queries, keys, (((1,), (1,)), ((), ())), preferred_element_type=F32
        ) * HD ** (-0.5)
        masked = jnp.where(may, scores, -1e30)
        row_max = jnp.max(masked, axis=1, keepdims=True)
        raised = jnp.where(may, jnp.exp(masked - row_max), 0.0)
        denom = jnp.sum(raised, axis=1, keepdims=True)
        denom = jnp.where(denom == 0.0, 1.0, denom)
        prob = (raised / denom).astype(BF16)
        probs[head] = prob
        total = total + lax.dot_general(
            prob, cot[:, head * HD : (head + 1) * HD], (((0,), (0,)), ((), ())),
            preferred_element_type=F32,
        )
    vc[...] = total.astype(BF16)

    vc_copy = remote(vc, vc_in, vcs, vcr, sibling, t)
    vc_copy.start()
    R[...] = jnp.dot(
        TH[c].reshape(NL * NL * PART, -1), vc[...], preferred_element_type=F32
    ).reshape(NL, NL * PART, HD)
    take_value(2)
    rows_copy.wait_recv()
    vc_copy.wait_recv()

    def both_cores(ks):
        lines = [(a + k) % NL for k in ks]
        rows = jnp.concatenate([TH_in[line].reshape(NL * PART, -1) for line in lines], axis=0)
        prod = jnp.dot(rows, vc_in[...], preferred_element_type=F32)
        return [
            R[line] + prod[i * NL * PART : (i + 1) * NL * PART] for i, line in enumerate(lines)
        ]

    def sum_copy(k):
        return remote(H.at[k], P1.at[k], q1s.at[k], q1r.at[k], first((a + k) % NL), t)

    sums = [sum_copy(k) for k in range(1, NL)]
    for ks in ((4,), (3, 5), (2, 6)):
        for k, value in zip(ks, both_cores(ks)):
            H[k] = value.astype(BF16)
            sum_copy(k).start()
    part1, part7, acc = both_cores((1, 7, 0))
    for k, value in ((1, part1), (7, part7)):
        H[k] = value.astype(BF16)
        sum_copy(k).start()
    take_value(3)
    for copy in sums:
        copy.wait_recv()
    for k in range(1, NL):
        acc = acc + P1[k].astype(F32)
    items = acc.reshape(NL, PART, HD)
    F[...] = jnp.concatenate([items, items[:, :8]], axis=1).astype(BF16)
    own_item[...] = jnp.sum(
        jnp.where(lax.broadcasted_iota(jnp.int32, (NL, 1, 1), 0) == b, items, 0.0), axis=0
    )
    last = []
    for k in (4, 3, 5, 2, 6, 1, 7):
        copy = remote(F.at[(b + k) % NL], P2.at[k], q2s.at[k], q2r.at[k], second((b + k) % NL), t)
        copy.start()
        last.append(copy)

    take_value(4)

    @pl.when(c == 0)
    def _():
        for part in value_shared:
            value_share(*part).wait_recv()

    values = jnp.zeros((GEN_BLK * BLK, HD), F32)
    for i in range(NL):
        values = values + lax.dot_general(
            NT[i].reshape(LINE, -1), V[i].reshape(LINE, HD), (((0,), (0,)), ((), ())),
            preferred_element_type=F32,
        )
    values = values.astype(BF16)
    for head in range(HEADS):
        att[:, head * HD : (head + 1) * HD] = jnp.dot(
            probs[head], values, preferred_element_type=F32
        ).astype(BF16)

    for copy in x_copies + sq_copies + sums + [sib_copy, tab_copy, fwd0, fwd1, rows_copy, vc_copy]:
        copy.wait_send()
    for i in range(7):
        along(i).wait_send()
    for k in range(NL):
        own_line(k, 0).wait_send()
        own_line(k, 1).wait_send()

    def all_left(core):
        for part in sent:
            ring(core, *part).wait_send()
        for s in range(4):
            for d in range(min(s + 1, 2)):
                to_sibling(core, d, s).wait_send()
        for j in range(4):
            last_to_sibling(core, j).wait_send()
        if core == 1:
            for k in range(1, NL):
                value_first(k).wait_send()
            for part in value_sent:
                value_ring(*part).wait_send()
            for part in value_shared:
                value_share(*part).wait_send()

    each_core(all_left)

    for copy in last:
        copy.wait_recv()
    out = own_item[...]
    for k in range(1, NL):
        out = out + P2[k].astype(F32)[:PART]
    grad[...] = out

    for copy in last:
        copy.wait_send()


def hand_over(att, grad, att_out, grad_out, att_held, grad_held, read, write):
    whole = pl.ds(0, PART)
    pieces = [(grad, grad_held, grad_out, whole)]
    for i in range(4):
        pieces.append((att, att_held, att_out, pl.ds(64 * i, 64)))
    reads = [
        pltpu.make_async_copy(source.at[rows], held.at[rows], read.at[i])
        for i, (source, held, _, rows) in enumerate(pieces)
    ]
    writes = [
        pltpu.make_async_copy(held.at[rows], target.at[rows], write.at[i])
        for i, (_, held, target, rows) in enumerate(pieces)
    ]
    for copy in reads:
        copy.start()
    for one, two in zip(reads, writes):
        one.wait()
        two.start()
    for copy in writes:
        copy.wait()


def shards(hidden_rows, cotangent, norm_gain, query_weight, key_weight, value_weight, source, segment, position):
    rows = GEN_BLK * BLK
    vmem = pl.BlockSpec(memory_space=pltpu.VMEM)
    dma = pltpu.SemaphoreType.DMA
    made = pl.pallas_call(
        kernel,
        out_shape=(
            jax.ShapeDtypeStruct((rows, HEADS * HD), BF16),
            jax.ShapeDtypeStruct((PART, HD), F32),
        ),
        in_specs=[pl.BlockSpec(memory_space=pltpu.HBM)] * 9,
        out_specs=(vmem, vmem),
        scratch_shapes=[
            pltpu.VMEM((rows, HEADS * HD), BF16),
            pltpu.VMEM((NT_X, 1, SLICE), F32),
            pltpu.VMEM((PART, HEADS * HD), BF16),
            pltpu.VMEM((PART, HD), BF16),
            pltpu.VMEM((PART, HD), BF16),
            pltpu.SMEM((CAP_BLK,), jnp.int32),
            pltpu.SMEM((CAP_BLK,), jnp.int32),
            pltpu.SMEM((CAP_BLK,), jnp.int32),
            pltpu.VMEM((2, NL, NL, CHIP, SW), BF16),
            pltpu.VMEM((NL, NL, CHIP, HD), BF16),
            pltpu.VMEM((NT_X, GEN_BLK, BLK, SLICE), BF16),
            pltpu.VMEM((NL, NL, CHIP, rows), BF16),
            pltpu.VMEM((PART, SW + HD), F32),
            pltpu.VMEM((PART, SW + HD), F32),
            pltpu.VMEM((8, 128), jnp.int32),
            pltpu.VMEM((8, 128), jnp.int32),
            pltpu.VMEM((2, rows, SW), F32),
            pltpu.VMEM((HEADS, rows, rows), BF16),
            pltpu.VMEM((rows, rows), jnp.int32),
            pltpu.VMEM((rows, HD), BF16),
            pltpu.VMEM((8, rows), F32),
            pltpu.VMEM((3, 8, rows), F32),
            pltpu.VMEM((rows, HD), F32),
            pltpu.VMEM((2, NL, NT_X, CHIP, rows), BF16),
            pltpu.VMEM((NL, NT_X, CHIP, rows), BF16),
            pltpu.VMEM((NL, CHIP, rows), F32),
            pltpu.VMEM((rows, HD), BF16),
            pltpu.VMEM((NL, NL * PART, HD), F32),
            pltpu.VMEM((NL, NL * PART, HD), BF16),
            pltpu.VMEM((NL, NL * PART, HD), BF16),
            pltpu.VMEM((NL, PART + 8, HD), BF16),
            pltpu.VMEM((NL, PART + 8, HD), BF16),
            pltpu.VMEM((PART, HD), F32),
            dma((10,)),
            dma, dma, dma, dma,
            dma((2, 2)), dma((2, 2)), dma((2,)), dma((2,)),
            dma((3,)), dma((3,)),
            dma((7,)), dma((7,)),
            dma((NL,)), dma((NL,)),
            dma((2, NL)),
            dma((2, 4, 4)), dma((2, 4, 4)),
            dma((2, 4)), dma((2, 4)),
            dma((2, 4)), dma((2, 4)), dma((4,)), dma((4,)),
            dma((2, 5)), dma((2, 5)),
            dma, dma, dma, dma,
            dma((NL,)), dma((NL,)), dma((NL,)), dma((NL,)),
        ],
        compiler_params=pltpu.CompilerParams(
            collective_id=0, has_side_effects=True, vmem_limit_bytes=60 * 1024 * 1024
        ),
    )(
        hidden_rows, cotangent, norm_gain.reshape(NT_X, 1, SLICE), query_weight, key_weight, value_weight,
        source, segment, position,
    )
    hbm = pl.BlockSpec(memory_space=pltpu.HBM)
    return pl.pallas_call(
        hand_over,
        out_shape=tuple(jax.ShapeDtypeStruct(one.shape, one.dtype) for one in made),
        in_specs=[hbm, hbm],
        out_specs=(hbm, hbm),
        scratch_shapes=[
            pltpu.VMEM(made[0].shape, BF16),
            pltpu.VMEM(made[1].shape, F32),
            dma((5,)),
            dma((5,)),
        ],
        compiler_params=pltpu.CompilerParams(vmem_limit_bytes=60 * 1024 * 1024),
    )(*made)


def solution(mesh):
    return jax.shard_map(
        shards,
        mesh=mesh,
        in_specs=(
            P("fsdp", "tp"),
            P("fsdp", "tp"),
            P(),
            P("fsdp", "tp"),
            P("fsdp", "tp"),
            P("fsdp", "tp"),
            P("fsdp"),
            P("fsdp"),
            P("fsdp"),
        ),
        out_specs=(P("fsdp", "tp"), P("fsdp", "tp")),
        check_vma=False,
    )
```
